256 devices in a mesh: ctx: 8 (over x_lo, y), req: 32 (over x_hi, z, core).
Axes of the slice: x: 4 (x_hi: 2, x_lo: 2; x = x_hi * 2 + x_lo), y: 4, z: 8, core: 2. Of those that a mesh axis runs over, the one named last changes fastest.
Arguments:
- queries: bfloat16 [16384, 1024], P(('ctx', 'req')), may hold values from -12 to 12
- suffix_keys: bfloat16 [16384, 128], P(('ctx', 'req')), may hold values from -10 to 10
- suffix_values: bfloat16 [16384, 128], P(('ctx', 'req')), may hold values from -6 to 6
- prefix_keys: bfloat16 [32768, 128], P(('ctx', 'req')), may hold values from -7.5 to 7.5
- prefix_values: bfloat16 [32768, 128], P(('ctx', 'req')), may hold values from -6 to 6
- slot_request: int32 [16384], P(('ctx', 'req')), may hold values from 0 to 64, as said below
Outputs:
- attended: bfloat16 [16384, 1024], P(('ctx', 'req'))
The draws below stay inside these ranges and needn't reach their ends.
Inputs may be any that keep to these rules, and one draw needn't show every extreme that they name: `slot_request`: on each device the live slots come first and hold requests numbered 0, 1, 2 and so on in order, the slots of a request consecutive; empty slots hold 64. The devices with one index of ctx hold 32 times their number of live slots together, and one of them has all 64 slots live. Numbering the live slots of the devices with one index of ctx in order of req index and then slot, and giving each to the req index equal to its number modulo the number of devices along req, every device is given exactly 32 slots.
All inputs are finite; a program needn't handle non-finite values.
Results may differ from the reference program's by a relative error of at most 0.017.
Values may be sent and summed in bfloat16 or wider, within the bound.
No kernel may reach another device: no remote copies, remote signals or barrier semaphores. Data moves between devices by JAX's collectives and lax.ppermute only.
A program may use at most 64 MiB of HBM per device.

```python
import math
from functools import partial
import jax
import jax.numpy as jnp
from jax import lax

H = 8
HD = 128
SLOT_DEV = 64
LIVE_DEV = 32
PREFIX = 32768
SLOTS = 16384
N_CTX = 8
N_REQ = 32


def draw_queries(key, part):
    key = jax.random.fold_in(key, 11)
    key_base = jax.random.fold_in(key, 0)
    return jnp.clip(2.0 * jax.random.normal(key_base, (SLOTS, H * HD), jnp.float32), -12.0, 12.0).astype(jnp.bfloat16)


def draw_prefix_keys(key, part):
    key = jax.random.fold_in(key, 12)
    key_base = jax.random.fold_in(key, 0)
    return jnp.clip(1.25 * jax.random.normal(key_base, (PREFIX, HD), jnp.float32), -7.5, 7.5).astype(jnp.bfloat16)


def draw_suffix_keys(key, part):
    key = jax.random.fold_in(key, 13)
    key_base = jax.random.fold_in(key, 0)
    return jnp.clip(1.7 * jax.random.normal(key_base, (SLOTS, HD), jnp.float32), -10.0, 10.0).astype(jnp.bfloat16)


def shuffle(subkey):
    return jax.random.permutation(subkey, N_REQ)


def draw_slot_request(key, part):
    key = jax.random.fold_in(key, 21)
    key_pairs, key_order, key_cuts = jax.random.split(key, 3)
    pair_count = N_REQ // 2
    offset_draw = jax.random.randint(key_pairs, (N_CTX, pair_count), 0, LIVE_DEV + 1)
    offset_draw = offset_draw.at[:, 0].set(LIVE_DEV)
    paired = jnp.stack([LIVE_DEV + offset_draw, LIVE_DEV - offset_draw], axis=-1).reshape(N_CTX, N_REQ)
    orders = jax.vmap(shuffle)(jax.random.split(key_order, N_CTX))
    live_count = jnp.take_along_axis(paired, orders, axis=1).astype(jnp.int32)
    slot_index = jnp.arange(SLOT_DEV, dtype=jnp.int32)
    cut_flags = (jax.random.randint(key_cuts, (N_CTX, N_REQ, SLOT_DEV), 0, 96) == 0) & (slot_index[None, None, :] > 0)
    request_id = jnp.cumsum(cut_flags.astype(jnp.int32), axis=-1)
    live_mask = slot_index[None, None, :] < live_count[..., None]
    slot_request = jnp.where(live_mask, request_id, SLOT_DEV).astype(jnp.int32)
    return slot_request.reshape(-1)


def shard_levels(key, dims, shards, least, top_value):
    loudness = 1.0
    for position, parts in shards:
        heights = jax.random.uniform(jax.random.fold_in(jax.random.fold_in(key, 6), position), (parts,), jnp.float32, least / len(shards), top_value / len(shards))
        loudness = loudness * jnp.repeat(jnp.exp(heights), dims[position] // parts).reshape((-1,) + (1,) * (len(dims) - 1 - position))
    return loudness


def scatter_about(stream_key, extent, deviation, limit, cuts=(), held_as=jnp.bfloat16):
    drawn = jax.random.normal(stream_key, extent, jnp.float32) * deviation
    if len(cuts) > 0:
        drawn = shard_levels(stream_key, extent, cuts, -0.22, 0.18) * drawn
    return jnp.clip(drawn, min=-limit, max=limit).astype(held_as)


def setup_inputs(seed: int = 0) -> dict:
    key_list = jax.random.split(jax.random.key(seed), 7)
    queries = draw_queries(jax.random.fold_in(key_list[6], 71), 0)
    suffix_keys = draw_suffix_keys(jax.random.fold_in(key_list[6], 71), 0)
    suffix_values = scatter_about(key_list[2], (SLOTS, HD), 1.0, 6.0, ((0, 256),))
    prefix_keys = draw_prefix_keys(jax.random.fold_in(key_list[6], 71), 0)
    prefix_values = scatter_about(key_list[4], (PREFIX, HD), 1.0, 6.0, ((0, 256),))
    slot_request = draw_slot_request(jax.random.fold_in(key_list[6], 71), 0)
    return dict(queries=queries, suffix_keys=suffix_keys, suffix_values=suffix_values, prefix_keys=prefix_keys, prefix_values=prefix_values, slot_request=slot_request)


MASKED_SCORE = -1e+30

def softmax_state(scores, value_rows):
    row_peak = lax.optimization_barrier(jnp.max(scores, axis=-1))
    weights = jnp.exp(scores - row_peak[..., None])
    mass_total = lax.optimization_barrier(jnp.sum(weights, axis=-1))
    rounded = lax.optimization_barrier(weights.astype(jnp.bfloat16))
    numerator = jnp.einsum('rhn,nd->rhd', rounded.astype(jnp.float32), value_rows)
    return (numerator, mass_total, row_peak)

def combine_states(prefix_part, suffix_part, live_mask):
    prefix_sum, prefix_mass, prefix_peak = prefix_part
    suffix_sum, suffix_mass, suffix_peak = suffix_part
    row_peak = jnp.maximum(prefix_peak, suffix_peak)
    prefix_factor = jnp.exp(prefix_peak - row_peak)
    suffix_factor = jnp.exp(suffix_peak - row_peak)
    upper = prefix_sum * prefix_factor[..., None] + suffix_sum * suffix_factor[..., None]
    lower = prefix_mass * prefix_factor + suffix_mass * suffix_factor
    merged = upper / lower[..., None]
    slot_count = merged.shape[0]
    merged = merged.reshape(slot_count, -1)
    return jnp.where(live_mask[:, None], merged, 0.0).astype(jnp.bfloat16)

def attend_device(operands, prefix_keys32, prefix_values32):
    queries, suffix_keys, suffix_values, requests = operands
    slot_count = queries.shape[0]
    score_scale = 1.0 / math.sqrt(HD)
    query_block = queries.astype(jnp.float32).reshape(slot_count, H, HD)
    prefix_scores = jnp.einsum('rhd,nd->rhn', query_block, prefix_keys32) * score_scale
    prefix_part = softmax_state(prefix_scores, prefix_values32)
    suffix_scores = jnp.einsum('rhd,nd->rhn', query_block, suffix_keys.astype(jnp.float32)) * score_scale
    query_index = lax.broadcasted_iota(jnp.int32, (slot_count, slot_count), 0)
    key_index = lax.broadcasted_iota(jnp.int32, (slot_count, slot_count), 1)
    visible = (requests[:, None] == requests[None, :]) & (key_index <= query_index)
    suffix_scores = jnp.where(visible[:, None, :], suffix_scores, MASKED_SCORE)
    suffix_part = softmax_state(suffix_scores, suffix_values.astype(jnp.float32))
    return combine_states(prefix_part, suffix_part, requests < slot_count)

def reference(queries, suffix_keys, suffix_values, prefix_keys, prefix_values, slot_request):
    device_count = queries.shape[0] // SLOT_DEV
    operands = (queries.reshape(device_count, SLOT_DEV, H * HD), suffix_keys.reshape(device_count, SLOT_DEV, HD), suffix_values.reshape(device_count, SLOT_DEV, HD), slot_request.reshape(device_count, SLOT_DEV))
    keys_wide = prefix_keys.astype(jnp.float32)
    values_wide = prefix_values.astype(jnp.float32)
    result = lax.map(partial(attend_device, prefix_keys32=keys_wide, prefix_values32=values_wide), operands)
    return result.reshape(device_count * SLOT_DEV, H * HD)
```

```python
import math

import jax
import jax.numpy as jnp
from jax import lax
from jax.experimental import pallas as pl
from jax.experimental.pallas import tpu as pltpu
from jax.sharding import PartitionSpec as P

H = 8
HD = 128
AXES = ("ctx", "req")
SCALE = 1.4426950408889634 / math.sqrt(HD)
MASKED_SCORE = -1e30
BLOCK = 128
POOL = 4
KEY_TILE = 512
ROW_TILE = 256
TILES_AT_ONCE = 4

f32, bf16 = jnp.float32, jnp.bfloat16
VMEM = pl.BlockSpec(memory_space=pltpu.VMEM)
PARAMS = pltpu.CompilerParams(vmem_limit_bytes=56 * 2**20)


def moved(array, place):
    pairs = []
    for x in range(4):
        for y in range(4):
            for z in range(8):
                for c in range(2):
                    pairs.append((linear(x, y, z, c), linear(*place(x, y, z, c))))
    return lax.ppermute(array, AXES, sorted(pairs))


def linear(x, y, z, c):
    return ((x % 2) * 4 + y) * 32 + (x // 2) * 16 + z * 2 + c


def by_xor(array, dx=0, dy=0, dz=0, dc=0):
    return moved(array, lambda x, y, z, c: (x ^ dx, y ^ dy, z ^ dz, c ^ dc))


def by_ring(array, dy=0, dz=0):
    return moved(array, lambda x, y, z, c: (x, (y + dy) % 4, (z + dz) % 8, c))


def wide(column_like, width):
    return jnp.concatenate([column_like] * (width // 128), axis=1)


def spread(column, rows):
    return jnp.broadcast_to(column, (rows, 128))


def queries_kernel(*refs):
    out = refs[-1]
    slots = refs[0].shape[0]
    for j, ref in enumerate(refs[:-1]):
        for h in range(H):
            scaled = ref[:, h * HD : (h + 1) * HD].astype(f32) * SCALE
            high = scaled.astype(bf16)
            low = (scaled - high.astype(f32)).astype(bf16)
            rows = pl.ds((j * H + h) * slots, slots)
            out[rows, 0:HD] = high
            out[rows, HD : 2 * HD] = low


def prepared_queries(pool):
    slots = pool[0].shape[0]
    return pl.pallas_call(
        queries_kernel,
        out_shape=jax.ShapeDtypeStruct((len(pool) * H * slots, 2 * HD), bf16),
        in_specs=[VMEM] * len(pool),
        out_specs=VMEM,
        compiler_params=PARAMS,
    )(*pool)


def load_pieces(pieces, keys, values):
    at = 0
    ones = jnp.ones((BLOCK, HD), bf16)
    for piece in pieces:
        for b in range(piece.shape[0]):
            rows = pl.ds(at, BLOCK)
            key_rows = piece[b, 0:BLOCK, :]
            keys[rows, 0:HD] = key_rows
            keys[rows, HD : 2 * HD] = key_rows
            values[rows, 0:HD] = piece[b, BLOCK : 2 * BLOCK, :]
            values[rows, HD : 2 * HD] = ones
            at += BLOCK
    return at


def fold_tiles(query, keys, values, key_count, total_in, peak_in, total, peak, first):
    row_count = query.shape[0]
    at_once = min(TILES_AT_ONCE, row_count // ROW_TILE)

    def step(i, _):
        for start in range(0, key_count, KEY_TILE):
            length = min(KEY_TILE, key_count - start)
            for u in range(at_once):
                rows = pl.ds(pl.multiple_of((i * at_once + u) * ROW_TILE, ROW_TILE), ROW_TILE)
                scores = lax.dot_general(
                    query[rows, :],
                    keys[pl.ds(start, length), :],
                    (((1,), (1,)), ((), ())),
                    preferred_element_type=f32,
                )
                block_peak = spread(jnp.max(scores, axis=1, keepdims=True), ROW_TILE)
                fresh = first and start == 0
                if fresh:
                    new_peak = block_peak
                else:
                    held_peak, held_total = (peak_in, total_in) if start == 0 else (peak, total)
                    old_peak = held_peak[rows, :]
                    new_peak = jnp.maximum(old_peak, block_peak)
                weights = jnp.exp2(scores - wide(new_peak, length)).astype(bf16)
                added = jnp.dot(weights, values[pl.ds(start, length), :], preferred_element_type=f32)
                if not fresh:
                    added = added + held_total[rows, :] * wide(jnp.exp2(old_peak - new_peak), 2 * HD)
                total[rows, :] = added
                peak[rows, :] = new_peak
        return 0

    lax.fori_loop(0, row_count // (ROW_TILE * at_once), step, 0)


def fold_kernel(piece_count, first, *refs):
    query, pieces = refs[0], refs[1 : 1 + piece_count]
    rest = refs[1 + piece_count :]
    if first:
        total, peak, keys, values = rest
        total_in = peak_in = None
    else:
        total_in, peak_in, total, peak, keys, values = rest
    key_count = load_pieces(pieces, keys, values)
    fold_tiles(query, keys, values, key_count, total_in, peak_in, total, peak, first)


def folded(query, pieces, state=None):
    first = state is None
    state = () if first else tuple(state)
    row_count = query.shape[0]
    key_count = sum(p.shape[0] for p in pieces) * BLOCK
    at = 1 + len(pieces)
    return pl.pallas_call(
        lambda *refs: fold_kernel(len(pieces), first, *refs),
        out_shape=(
            jax.ShapeDtypeStruct((row_count, 2 * HD), f32),
            jax.ShapeDtypeStruct((row_count, HD), f32),
        ),
        in_specs=[VMEM] * (at + len(state)),
        out_specs=(VMEM, VMEM),
        scratch_shapes=[pltpu.VMEM((key_count, 2 * HD), bf16)] * 2,
        input_output_aliases={} if first else {at: 0, at + 1: 1},
        compiler_params=PARAMS,
    )(query, *pieces, *state)


def message_kernel(total, peak, *outs):
    slots = outs[0].shape[0]
    lane = lax.broadcasted_iota(jnp.int32, (slots, 128), 1)
    for j, out in enumerate(outs):
        packed = jnp.zeros((slots, 128), f32)
        for h in range(H):
            rows = pl.ds((j * H + h) * slots, slots)
            mass = total[rows, HD : 2 * HD]
            out[:, h * HD : (h + 1) * HD] = (total[rows, 0:HD] / mass).astype(bf16)
            level = peak[rows, :] + jnp.log2(mass)
            one = level.astype(bf16).astype(f32)
            two = (level - one).astype(bf16).astype(f32)
            three = level - one - two
            term = jnp.where(lane % 16 == 0, one, jnp.where(lane % 16 == 1, two, three))
            packed = jnp.where((lane // 16 == h) & (lane % 16 < 3), term, packed)
        out[:, H * HD :] = packed.astype(bf16)


def messages(state, slots):
    total, peak = state
    count = total.shape[0] // (H * slots)
    return pl.pallas_call(
        message_kernel,
        out_shape=tuple(jax.ShapeDtypeStruct((slots, H * HD + 128), bf16) for _ in range(count)),
        in_specs=[VMEM, VMEM],
        out_specs=tuple([VMEM] * count),
        compiler_params=PARAMS,
    )(total, peak)


def request_column(request_row, slots):
    row = lax.broadcasted_iota(jnp.int32, (slots, slots), 0)
    column = lax.broadcasted_iota(jnp.int32, (slots, slots), 1)
    across = jnp.broadcast_to(request_row, (slots, slots))
    return jnp.sum(jnp.where(row == column, across, 0), axis=1, keepdims=True), across, row, column


def suffix_kernel(queries, key_rows, value_rows, request, quotient, level):
    slots = queries.shape[0]
    own, across, row, column = request_column(request[...], slots)
    visible = (own == across) & (column <= row)
    for h in range(H):
        scores = lax.dot_general(
            queries[:, h * HD : (h + 1) * HD],
            key_rows[...],
            (((1,), (1,)), ((), ())),
            preferred_element_type=f32,
        )
        scores = jnp.where(visible, scores * SCALE, MASKED_SCORE)
        peak = jnp.max(scores, axis=1, keepdims=True)
        weights = jnp.exp2(scores - peak)
        mass = jnp.sum(weights, axis=1, keepdims=True)
        total = jnp.dot(weights.astype(bf16), value_rows[...], preferred_element_type=f32)
        rows = pl.ds(h * slots, slots)
        quotient[rows, :] = total / mass
        level[rows, :] = spread(peak + jnp.log2(mass), slots)


def suffix_part(queries, suffix_keys, suffix_values, request_row):
    shape = jax.ShapeDtypeStruct((H * queries.shape[0], HD), f32)
    return pl.pallas_call(
        suffix_kernel,
        out_shape=(shape, shape),
        in_specs=[VMEM] * 4,
        out_specs=(VMEM, VMEM),
        compiler_params=PARAMS,
    )(queries, suffix_keys, suffix_values, request_row)


def combine_kernel(*refs):
    parts, suffix_quotient, suffix_level, request, out = refs[:-4], *refs[-4:]
    slots = out.shape[0]
    own = request_column(request[...], slots)[0]
    live = jnp.broadcast_to(own < slots, (slots, HD))
    lane = lax.broadcasted_iota(jnp.int32, (128, H * HD), 0)
    column = lax.broadcasted_iota(jnp.int32, (128, H * HD), 1)
    gather = ((lane // 16 == column // HD) & (lane % 16 < 3)).astype(bf16)
    levels = [
        jnp.dot(part[:, H * HD :], gather, preferred_element_type=f32) for part in parts
    ]
    for h in range(H):
        columns = slice(h * HD, (h + 1) * HD)
        rows = pl.ds(h * slots, slots)
        all_levels = [level[:, columns] for level in levels] + [suffix_level[rows, :]]
        all_quotients = [part[:, columns].astype(f32) for part in parts]
        all_quotients.append(suffix_quotient[rows, :])
        top = all_levels[0]
        for level in all_levels[1:]:
            top = jnp.maximum(top, level)
        upper = lower = 0.0
        for level, quotient in zip(all_levels, all_quotients):
            weight = jnp.exp2(level - top)
            upper = upper + weight * quotient
            lower = lower + weight
        out[:, columns] = jnp.where(live, upper / lower, 0.0).astype(bf16)


def combined(parts, suffix, request_row):
    slots = parts[0].shape[0]
    return pl.pallas_call(
        combine_kernel,
        out_shape=jax.ShapeDtypeStruct((slots, H * HD), bf16),
        in_specs=[VMEM] * (len(parts) + 3),
        out_specs=VMEM,
        compiler_params=PARAMS,
    )(*parts, *suffix, request_row)


def per_device(queries, suffix_keys, suffix_values, prefix_keys, prefix_values, slot_request):
    slots = queries.shape[0]
    request_row = slot_request.reshape(1, slots)
    own = jnp.concatenate([prefix_keys, prefix_values], axis=0)[None]

    far = [by_xor(own, dz=4), by_ring(own, dz=2), by_ring(own, dz=-2)]
    pool = [
        queries,
        by_xor(queries, dx=1),
        by_xor(queries, dz=1),
        by_xor(queries, dx=1, dz=1),
    ]
    first = jnp.concatenate([own, *far], axis=0)
    suffix = suffix_part(queries, suffix_keys, suffix_values, request_row)
    query = prepared_queries(pool)

    half_a, half_b = first[:2], first[2:]
    a_x = by_xor(half_a, dx=2)
    b_y = [by_ring(half_b, dy=1), by_ring(half_b, dy=-1), by_xor(half_b, dy=2)]
    first_c = by_xor(first, dc=1)
    state = folded(query, [first])

    second_a = jnp.concatenate([half_a, a_x], axis=0)
    second_b = jnp.concatenate([half_b, *b_y], axis=0)
    a_y = [by_ring(second_a, dy=1), by_ring(second_a, dy=-1), by_xor(second_a, dy=2)]
    b_x = by_xor(second_b, dx=2)
    second = [a_x, *b_y]
    second_c = by_xor(jnp.concatenate(second, axis=0), dc=1)
    state = folded(query, [first_c, *second], state)

    third_c = by_xor(jnp.concatenate(a_y[:2], axis=0), dc=1)
    state = folded(query, [second_c, *a_y[:2]], state)
    last = [a_y[2], b_x]
    last_c = by_xor(jnp.concatenate(last, axis=0), dc=1)
    state = folded(query, [third_c, *last], state)
    state = folded(query, [last_c], state)

    parts = messages(state, slots)
    parts = [
        parts[0],
        by_xor(parts[1], dx=1),
        by_xor(parts[2], dz=1),
        by_xor(parts[3], dx=1, dz=1),
    ]
    return combined(parts, suffix, request_row)


def solution(mesh):
    placed = (
        P(AXES, None),
        P(AXES, None),
        P(AXES, None),
        P(AXES, None),
        P(AXES, None),
        P(AXES),
    )
    return jax.shard_map(
        per_device, mesh=mesh, in_specs=placed, out_specs=P(AXES, None), check_vma=False
    )
```

```python
import math

import jax
import jax.numpy as jnp
from jax import lax
from jax.experimental import pallas as pl
from jax.experimental.pallas import tpu as pltpu
from jax.sharding import PartitionSpec as P

H = 8
HD = 128
AXES = ("ctx", "req")
SCALE = 1.4426950408889634 / math.sqrt(HD)
MASKED_SCORE = -1e30
BLOCK = 128
POOL = 4
KEY_TILE = 512
ROW_TILE = 256
MASS_LIMIT = 2.0**100

f32, bf16 = jnp.float32, jnp.bfloat16
VMEM = pl.BlockSpec(memory_space=pltpu.VMEM)
PARAMS = pltpu.CompilerParams(vmem_limit_bytes=24 * 2**20)


def moved(array, place):
    pairs = []
    for x in range(4):
        for y in range(4):
            for z in range(8):
                for c in range(2):
                    pairs.append((linear(x, y, z, c), linear(*place(x, y, z, c))))
    return lax.ppermute(array, AXES, sorted(pairs))


def linear(x, y, z, c):
    return ((x % 2) * 4 + y) * 32 + (x // 2) * 16 + z * 2 + c


def by_xor(array, dx=0, dy=0, dz=0, dc=0):
    return moved(array, lambda x, y, z, c: (x ^ dx, y ^ dy, z ^ dz, c ^ dc))


def by_ring(array, dy=0, dz=0):
    return moved(array, lambda x, y, z, c: (x, (y + dy) % 4, (z + dz) % 8, c))


def wide(column_like, width):
    return jnp.concatenate([column_like] * (width // 128), axis=1)


def spread(column, rows):
    return jnp.broadcast_to(column, (rows, 128))


def prepare(source, out):
    slots = source.shape[0]
    for h in range(H):
        scaled = source[:, h * HD : (h + 1) * HD].astype(f32) * SCALE
        high = scaled.astype(bf16)
        low = (scaled - high.astype(f32)).astype(bf16)
        rows = pl.ds(h * slots, slots)
        out[rows, 0:HD] = high
        out[rows, HD : 2 * HD] = low


def scored(query, keys):
    return lax.dot_general(query, keys, (((1,), (1,)), ((), ())), preferred_element_type=f32)


def request_column(request_row, slots):
    row = lax.broadcasted_iota(jnp.int32, (slots, slots), 0)
    column = lax.broadcasted_iota(jnp.int32, (slots, slots), 1)
    across = jnp.broadcast_to(request_row, (slots, slots))
    return jnp.sum(jnp.where(row == column, across, 0), axis=1, keepdims=True), across, row, column


def cost(rows, keys):
    return pl.CostEstimate(
        flops=8 * rows * keys * HD, transcendentals=rows * keys, bytes_accessed=2048 * rows
    )


def own_kernel(queries, suffix_keys, suffix_values, request, query, quotient, level):
    slots = queries.shape[0]
    prepare(queries, query)
    own, across, row, column = request_column(request[...], slots)
    visible = ((own == across) & (column <= row)).astype(jnp.int32)
    visible = jnp.concatenate([visible] * H, axis=0) == 1
    key_rows = jnp.concatenate([suffix_keys[...]] * 2, axis=1)
    scores = jnp.where(visible, scored(query[...], key_rows), MASKED_SCORE)
    peak = jnp.max(scores, axis=1, keepdims=True)
    weights = jnp.exp2(scores - peak).astype(bf16)
    value_rows = jnp.concatenate([suffix_values[...], jnp.ones((slots, HD), bf16)], axis=1)
    total = jnp.dot(weights, value_rows, preferred_element_type=f32)
    mass = total[:, HD:]
    quotient[...] = total[:, :HD] / mass
    level[...] = spread(peak, H * slots) + jnp.log2(mass)


def own_part(queries, suffix_keys, suffix_values, request_row):
    slots = queries.shape[0]
    shape = jax.ShapeDtypeStruct((H * slots, HD), f32)
    return pl.pallas_call(
        own_kernel,
        out_shape=(jax.ShapeDtypeStruct((H * slots, 2 * HD), bf16), shape, shape),
        in_specs=[VMEM] * 4,
        out_specs=(VMEM,) * 3,
        compiler_params=PARAMS,
        cost_estimate=cost(H * slots, 512),
    )(queries, suffix_keys, suffix_values, request_row)


def load_pieces(pieces, keys, values):
    at = 0
    ones = jnp.ones((BLOCK, HD), bf16)
    for piece in pieces:
        for b in range(piece.shape[0]):
            rows = pl.ds(at, BLOCK)
            key_rows = piece[b, 0:BLOCK, :]
            keys[rows, 0:HD] = key_rows
            keys[rows, HD : 2 * HD] = key_rows
            values[rows, 0:HD] = piece[b, BLOCK : 2 * BLOCK, :]
            values[rows, HD : 2 * HD] = ones
            at += BLOCK
    return at


def first_kernel(*refs):
    query, refs = refs[0], refs[1:]
    others, piece, refs = refs[: POOL - 1], refs[POOL - 1], refs[POOL:]
    prepared, totals, peaks = refs[: POOL - 1], refs[POOL - 1 : 2 * POOL - 1], refs[2 * POOL - 1 : 3 * POOL - 1]
    keys, values = refs[3 * POOL - 1 :]
    key_count = load_pieces([piece], keys, values)
    for source, out in zip(others, prepared):
        prepare(source, out)
    for j, held in enumerate([query, *prepared]):
        for start in range(0, held.shape[0], ROW_TILE):
            rows = pl.ds(start, ROW_TILE)
            scores = scored(held[rows, :], keys[...])
            peak = spread(jnp.max(scores, axis=1, keepdims=True), ROW_TILE)
            weights = jnp.exp2(scores - wide(peak, key_count)).astype(bf16)
            totals[j][rows, :] = jnp.dot(weights, values[...], preferred_element_type=f32)
            peaks[j][rows, :] = peak


def first_fold(query, others, piece):
    rows, key_count = query.shape[0], piece.shape[0] * BLOCK
    shapes = (
        [jax.ShapeDtypeStruct((rows, 2 * HD), bf16)] * (POOL - 1)
        + [jax.ShapeDtypeStruct((rows, 2 * HD), f32)] * POOL
        + [jax.ShapeDtypeStruct((rows, HD), f32)] * POOL
    )
    outs = pl.pallas_call(
        first_kernel,
        out_shape=tuple(shapes),
        in_specs=[VMEM] * (POOL + 1),
        out_specs=(VMEM,) * len(shapes),
        scratch_shapes=[pltpu.VMEM((key_count, 2 * HD), bf16)] * 2,
        compiler_params=PARAMS,
        cost_estimate=cost(POOL * rows, key_count + 512),
    )(query, *others, piece)
    return [query, *outs[: POOL - 1]], outs[POOL - 1 : 2 * POOL - 1], outs[2 * POOL - 1 :]


def add_tile(query, total, peak, keys, values, rows, span):
    weights = jnp.exp2(scored(query[rows, :], keys[span, :]) - wide(peak[rows, :], KEY_TILE))
    total[rows, :] += jnp.dot(weights.astype(bf16), values[span, :], preferred_element_type=f32)


def fold_kernel(piece_count, *refs):
    queries, peaks, refs = refs[:POOL], refs[POOL : 2 * POOL], refs[2 * POOL :]
    pieces, refs = refs[:piece_count], refs[piece_count:]
    totals, (keys, values) = refs[POOL : 2 * POOL], refs[2 * POOL :]
    for held, total in zip(refs[:POOL], totals):
        total[...] = held[...]
    key_count = load_pieces(pieces, keys, values)

    def step(i, _):
        span = pl.ds(pl.multiple_of(i * KEY_TILE, KEY_TILE), KEY_TILE)
        for j in range(POOL):
            for start in range(0, queries[j].shape[0], ROW_TILE):
                add_tile(queries[j], totals[j], peaks[j], keys, values, pl.ds(start, ROW_TILE), span)
        return 0

    lax.fori_loop(0, key_count // KEY_TILE, step, 0)


def folded(queries, peaks, totals, pieces):
    rows = queries[0].shape[0]
    key_count = sum(p.shape[0] for p in pieces) * BLOCK
    assert key_count % KEY_TILE == 0
    at = 2 * POOL + len(pieces)
    return pl.pallas_call(
        lambda *refs: fold_kernel(len(pieces), *refs),
        out_shape=(jax.ShapeDtypeStruct((rows, 2 * HD), f32),) * POOL,
        in_specs=[VMEM] * (at + POOL),
        out_specs=(VMEM,) * POOL,
        scratch_shapes=[pltpu.VMEM((key_count, 2 * HD), bf16)] * 2,
        input_output_aliases={at + j: j for j in range(POOL)},
        compiler_params=PARAMS,
        cost_estimate=cost(POOL * rows, key_count),
    )(*queries, *peaks, *pieces, *totals)


def refold(query, total, peak, blocks, every, semaphore):
    at = 0
    for piece in every:
        copy = pltpu.make_async_copy(piece, blocks.at[pl.ds(at, piece.shape[0])], semaphore)
        copy.start()
        copy.wait()
        at += piece.shape[0]
    total[...] = jnp.zeros_like(total)
    peak[...] = jnp.full(peak.shape, MASKED_SCORE, f32)
    rows = query.shape[0]
    ones = jnp.ones((BLOCK, HD), bf16)

    def step(b, _):
        key_rows = blocks[b, 0:BLOCK, :]
        scores = scored(query[...], jnp.concatenate([key_rows, key_rows], axis=1))
        old = peak[...]
        new = jnp.maximum(old, spread(jnp.max(scores, axis=1, keepdims=True), rows))
        weights = jnp.exp2(scores - new).astype(bf16)
        value_rows = jnp.concatenate([blocks[b, BLOCK : 2 * BLOCK, :], ones], axis=1)
        added = jnp.dot(weights, value_rows, preferred_element_type=f32)
        total[...] = total[...] * wide(jnp.exp2(old - new), 2 * HD) + added
        peak[...] = new
        return 0

    lax.fori_loop(0, at, step, 0)


def last_kernel(piece_count, every_count, *refs):
    query, peak_in, total_in, refs = refs[0], refs[1], refs[2], refs[3:]
    pieces, every, refs = refs[:piece_count], refs[piece_count:][:every_count], refs[piece_count + every_count :]
    out, total, peak, keys, values, blocks, semaphore = refs
    slots = out.shape[0]
    key_count = load_pieces(pieces, keys, values)
    total[...] = total_in[...]
    peak[...] = peak_in[...]
    for key_start in range(0, key_count, KEY_TILE):
        for start in range(0, query.shape[0], ROW_TILE):
            add_tile(query, total, peak, keys, values, pl.ds(start, ROW_TILE), pl.ds(key_start, KEY_TILE))

    @pl.when(jnp.logical_not(jnp.max(total[:, HD:]) < MASS_LIMIT))
    def _():
        refold(query, total, peak, blocks, every, semaphore)

    lane = lax.broadcasted_iota(jnp.int32, (slots, 128), 1)
    packed = jnp.zeros((slots, 128), f32)
    for h in range(H):
        rows = pl.ds(h * slots, slots)
        mass = total[rows, HD : 2 * HD]
        out[:, h * HD : (h + 1) * HD] = (total[rows, 0:HD] / mass).astype(bf16)
        level = peak[rows, :] + jnp.log2(mass)
        one = level.astype(bf16).astype(f32)
        two = (level - one).astype(bf16).astype(f32)
        three = level - one - two
        term = jnp.where(lane % 16 == 0, one, jnp.where(lane % 16 == 1, two, three))
        packed = jnp.where((lane // 16 == h) & (lane % 16 < 3), term, packed)
    out[:, H * HD :] = packed.astype(bf16)


def last_fold(query, peak, total, pieces, every):
    rows = query.shape[0]
    slots = rows // H
    key_count = sum(p.shape[0] for p in pieces) * BLOCK
    block_count = sum(p.shape[0] for p in every)
    return pl.pallas_call(
        lambda *refs: last_kernel(len(pieces), len(every), *refs),
        out_shape=jax.ShapeDtypeStruct((slots, H * HD + 128), bf16),
        in_specs=[VMEM] * (3 + len(pieces)) + [pl.BlockSpec(memory_space=pl.ANY)] * len(every),
        out_specs=VMEM,
        scratch_shapes=[
            pltpu.VMEM((rows, 2 * HD), f32),
            pltpu.VMEM((rows, HD), f32),
            pltpu.VMEM((key_count, 2 * HD), bf16),
            pltpu.VMEM((key_count, 2 * HD), bf16),
            pltpu.VMEM((block_count, 2 * BLOCK, HD), bf16),
            pltpu.SemaphoreType.DMA,
        ],
        compiler_params=PARAMS,
        cost_estimate=cost(rows, key_count),
    )(query, peak, total, *pieces, *every)


def combine_kernel(*refs):
    parts, suffix_quotient, suffix_level, request, out = refs[:-4], *refs[-4:]
    slots = out.shape[0]
    own = request_column(request[...], slots)[0]
    live = jnp.broadcast_to(own < slots, (slots, HD))
    lane = lax.broadcasted_iota(jnp.int32, (128, H * HD), 0)
    column = lax.broadcasted_iota(jnp.int32, (128, H * HD), 1)
    gather = ((lane // 16 == column // HD) & (lane % 16 < 3)).astype(bf16)
    levels = [
        jnp.dot(part[:, H * HD :], gather, preferred_element_type=f32) for part in parts
    ]
    for h in range(H):
        columns = slice(h * HD, (h + 1) * HD)
        rows = pl.ds(h * slots, slots)
        all_levels = [level[:, columns] for level in levels] + [suffix_level[rows, :]]
        all_quotients = [part[:, columns].astype(f32) for part in parts]
        all_quotients.append(suffix_quotient[rows, :])
        top = all_levels[0]
        for level in all_levels[1:]:
            top = jnp.maximum(top, level)
        upper = lower = 0.0
        for level, quotient in zip(all_levels, all_quotients):
            weight = jnp.exp2(level - top)
            upper = upper + weight * quotient
            lower = lower + weight
        out[:, columns] = jnp.where(live, upper / lower, 0.0).astype(bf16)


def combined(parts, suffix, request_row):
    slots = parts[0].shape[0]
    return pl.pallas_call(
        combine_kernel,
        out_shape=jax.ShapeDtypeStruct((slots, H * HD), bf16),
        in_specs=[VMEM] * (len(parts) + 3),
        out_specs=VMEM,
        compiler_params=PARAMS,
    )(*parts, *suffix, request_row)


def per_device(queries, suffix_keys, suffix_values, prefix_keys, prefix_values, slot_request):
    slots = queries.shape[0]
    request_row = slot_request.reshape(1, slots)
    own = jnp.concatenate([prefix_keys, prefix_values], axis=0)[None]

    far = [by_xor(own, dz=4), by_ring(own, dz=2), by_ring(own, dz=-2)]
    others = [
        by_xor(queries, dx=1, dz=1),
        by_xor(queries, dx=1),
        by_xor(queries, dz=1),
    ]
    query, *suffix = own_part(queries, suffix_keys, suffix_values, request_row)
    first = jnp.concatenate([own, *far], axis=0)

    half_a, half_b = first[:2], first[2:]
    a_x = by_xor(half_a, dx=2)
    b_y = [by_ring(half_b, dy=1), by_ring(half_b, dy=-1), by_xor(half_b, dy=2)]
    first_c = by_xor(first, dc=1)
    pool, totals, peaks = first_fold(query, others, first)

    second_a = jnp.concatenate([half_a, a_x], axis=0)
    second_b = jnp.concatenate([half_b, *b_y], axis=0)
    a_y = [by_ring(second_a, dy=1), by_ring(second_a, dy=-1), by_xor(second_a, dy=2)]
    b_x = by_xor(second_b, dx=2)
    second = [a_x, *b_y]
    second_c = by_xor(jnp.concatenate(second, axis=0), dc=1)
    totals = folded(pool, peaks, totals, [first_c, *second])

    third_c = by_xor(jnp.concatenate(a_y[:2], axis=0), dc=1)
    totals = folded(pool, peaks, totals, [second_c, *a_y[:2]])
    last = [a_y[2], b_x]
    last_c = by_xor(jnp.concatenate(last, axis=0), dc=1)
    totals = folded(pool, peaks, totals, [third_c, *last])

    every = [first, first_c, *second, second_c, *a_y[:2], third_c, *last, last_c]
    parts = []
    for j in (1, 2, 3, 0):
        parts.append(last_fold(pool[j], peaks[j], totals[j], [last_c], every))
    parts = [
        parts[3],
        by_xor(parts[0], dx=1, dz=1),
        by_xor(parts[1], dx=1),
        by_xor(parts[2], dz=1),
    ]
    return combined(parts, suffix, request_row)


def solution(mesh):
    placed = (
        P(AXES, None),
        P(AXES, None),
        P(AXES, None),
        P(AXES, None),
        P(AXES, None),
        P(AXES),
    )
    return jax.shard_map(
        per_device, mesh=mesh, in_specs=placed, out_specs=P(AXES, None), check_vma=False
    )
```

```python
import math

import jax
import jax.numpy as jnp
from jax import lax
from jax.experimental import pallas as pl
from jax.experimental.pallas import tpu as pltpu
from jax.sharding import PartitionSpec as P

H = 8
HD = 128
AXES = ("ctx", "req")
SCALE = 1.4426950408889634 / math.sqrt(HD)
MASKED_SCORE = -1e30
BLOCK = 128
POOL = 4
KEY_TILE = 512
ROW_TILE = 256
MASS_LIMIT = 2.0**100

f32, bf16 = jnp.float32, jnp.bfloat16
VMEM = pl.BlockSpec(memory_space=pltpu.VMEM)
PARAMS = pltpu.CompilerParams(vmem_limit_bytes=24 * 2**20)


def moved(array, place):
    pairs = []
    for x in range(4):
        for y in range(4):
            for z in range(8):
                for c in range(2):
                    pairs.append((linear(x, y, z, c), linear(*place(x, y, z, c))))
    return lax.ppermute(array, AXES, sorted(pairs))


def linear(x, y, z, c):
    return ((x % 2) * 4 + y) * 32 + (x // 2) * 16 + z * 2 + c


def by_xor(array, dx=0, dy=0, dz=0, dc=0):
    return moved(array, lambda x, y, z, c: (x ^ dx, y ^ dy, z ^ dz, c ^ dc))


def by_ring(array, dy=0, dz=0):
    return moved(array, lambda x, y, z, c: (x, (y + dy) % 4, (z + dz) % 8, c))


def wide(column_like, width):
    return jnp.concatenate([column_like] * (width // 128), axis=1)


def spread(column, rows):
    return jnp.broadcast_to(column, (rows, 128))


def prepare(source, out):
    slots = source.shape[0]
    for h in range(H):
        scaled = source[:, h * HD : (h + 1) * HD].astype(f32) * SCALE
        high = scaled.astype(bf16)
        low = (scaled - high.astype(f32)).astype(bf16)
        rows = pl.ds(h * slots, slots)
        out[rows, 0:HD] = high
        out[rows, HD : 2 * HD] = low


def scored(query, keys):
    return lax.dot_general(query, keys, (((1,), (1,)), ((), ())), preferred_element_type=f32)


def request_column(request_row, slots):
    row = lax.broadcasted_iota(jnp.int32, (slots, slots), 0)
    column = lax.broadcasted_iota(jnp.int32, (slots, slots), 1)
    across = jnp.broadcast_to(request_row, (slots, slots))
    return jnp.sum(jnp.where(row == column, across, 0), axis=1, keepdims=True), across, row, column


def cost(rows, keys):
    return pl.CostEstimate(
        flops=8 * rows * keys * HD, transcendentals=rows * keys, bytes_accessed=2048 * rows
    )


def own_kernel(*refs):
    sources, (query, quotient, level), held, semaphores = refs[:4], refs[4:7], refs[7:11], refs[11]
    copies = [pltpu.make_async_copy(a, b, semaphores.at[i]) for i, (a, b) in enumerate(zip(sources, held))]
    for copy in copies:
        copy.start()
    for copy in copies:
        copy.wait()
    queries, suffix_keys, suffix_values, request = held
    slots = queries.shape[0]
    prepare(queries, query)
    own, across, row, column = request_column(request[...], slots)
    visible = ((own == across) & (column <= row)).astype(jnp.int32)
    visible = jnp.concatenate([visible] * H, axis=0) == 1
    key_rows = jnp.concatenate([suffix_keys[...]] * 2, axis=1)
    scores = jnp.where(visible, scored(query[...], key_rows), MASKED_SCORE)
    peak = jnp.max(scores, axis=1, keepdims=True)
    weights = jnp.exp2(scores - peak).astype(bf16)
    value_rows = jnp.concatenate([suffix_values[...], jnp.ones((slots, HD), bf16)], axis=1)
    total = jnp.dot(weights, value_rows, preferred_element_type=f32)
    mass = total[:, HD:]
    quotient[...] = total[:, :HD] / mass
    level[...] = spread(peak, H * slots) + jnp.log2(mass)


def own_part(queries, suffix_keys, suffix_values, request_row):
    slots = queries.shape[0]
    shape = jax.ShapeDtypeStruct((H * slots, HD), f32)
    return pl.pallas_call(
        own_kernel,
        out_shape=(jax.ShapeDtypeStruct((H * slots, 2 * HD), bf16), shape, shape),
        in_specs=[pl.BlockSpec(memory_space=pl.ANY)] * 4,
        out_specs=(VMEM,) * 3,
        scratch_shapes=[
            pltpu.VMEM(a.shape, a.dtype) for a in (queries, suffix_keys, suffix_values, request_row)
        ]
        + [pltpu.SemaphoreType.DMA((4,))],
        compiler_params=PARAMS,
        cost_estimate=cost(H * slots, 512),
    )(queries, suffix_keys, suffix_values, request_row)


def load_pieces(pieces, keys, values):
    at = 0
    ones = jnp.ones((BLOCK, HD), bf16)
    for piece in pieces:
        for b in range(piece.shape[0]):
            rows = pl.ds(at, BLOCK)
            key_rows = piece[b, 0:BLOCK, :]
            keys[rows, 0:HD] = key_rows
            keys[rows, HD : 2 * HD] = key_rows
            values[rows, 0:HD] = piece[b, BLOCK : 2 * BLOCK, :]
            values[rows, HD : 2 * HD] = ones
            at += BLOCK
    return at


def first_kernel(*refs):
    query, refs = refs[0], refs[1:]
    others, piece, refs = refs[: POOL - 1], refs[POOL - 1], refs[POOL:]
    prepared, totals, peaks = refs[: POOL - 1], refs[POOL - 1 : 2 * POOL - 1], refs[2 * POOL - 1 : 3 * POOL - 1]
    keys, values = refs[3 * POOL - 1 :]
    key_count = load_pieces([piece], keys, values)
    for source, out in zip(others, prepared):
        prepare(source, out)
    for j, held in enumerate([query, *prepared]):
        for start in range(0, held.shape[0], ROW_TILE):
            rows = pl.ds(start, ROW_TILE)
            scores = scored(held[rows, :], keys[...])
            peak = spread(jnp.max(scores, axis=1, keepdims=True), ROW_TILE)
            weights = jnp.exp2(scores - wide(peak, key_count)).astype(bf16)
            totals[j][rows, :] = jnp.dot(weights, values[...], preferred_element_type=f32)
            peaks[j][rows, :] = peak


def first_fold(query, others, piece):
    rows, key_count = query.shape[0], piece.shape[0] * BLOCK
    shapes = (
        [jax.ShapeDtypeStruct((rows, 2 * HD), bf16)] * (POOL - 1)
        + [jax.ShapeDtypeStruct((rows, 2 * HD), f32)] * POOL
        + [jax.ShapeDtypeStruct((rows, HD), f32)] * POOL
    )
    outs = pl.pallas_call(
        first_kernel,
        out_shape=tuple(shapes),
        in_specs=[VMEM] * (POOL + 1),
        out_specs=(VMEM,) * len(shapes),
        scratch_shapes=[pltpu.VMEM((key_count, 2 * HD), bf16)] * 2,
        compiler_params=PARAMS,
        cost_estimate=cost(POOL * rows, key_count + 512),
    )(query, *others, piece)
    return [query, *outs[: POOL - 1]], list(outs[POOL - 1 : 2 * POOL - 1]), outs[2 * POOL - 1 :]


def add_tile(query, total, peak, keys, values, rows, start, length=KEY_TILE):
    span = pl.ds(start, length)
    weights = jnp.exp2(scored(query[rows, :], keys[span, :]) - wide(peak[rows, :], length))
    total[rows, :] += jnp.dot(weights.astype(bf16), values[span, :], preferred_element_type=f32)


def fold_kernel(piece_count, *refs):
    queries, peaks, refs = refs[:POOL], refs[POOL : 2 * POOL], refs[2 * POOL :]
    pieces, refs = refs[:piece_count], refs[piece_count:]
    totals, (keys, values) = refs[POOL : 2 * POOL], refs[2 * POOL :]
    for held, total in zip(refs[:POOL], totals):
        total[...] = held[...]
    key_count = load_pieces(pieces, keys, values)

    def add_all(key_start, length):
        for j in range(POOL):
            for start in range(0, queries[j].shape[0], ROW_TILE):
                rows = pl.ds(start, ROW_TILE)
                add_tile(queries[j], totals[j], peaks[j], keys, values, rows, key_start, length)

    def step(i, _):
        add_all(pl.multiple_of(i * KEY_TILE, KEY_TILE), KEY_TILE)
        return 0

    lax.fori_loop(0, key_count // KEY_TILE, step, 0)
    if key_count % KEY_TILE:
        add_all(key_count - key_count % KEY_TILE, key_count % KEY_TILE)


def folded(queries, peaks, totals, pieces):
    rows = queries[0].shape[0]
    key_count = sum(p.shape[0] for p in pieces) * BLOCK
    at = 2 * POOL + len(pieces)
    return pl.pallas_call(
        lambda *refs: fold_kernel(len(pieces), *refs),
        out_shape=(jax.ShapeDtypeStruct((rows, 2 * HD), f32),) * POOL,
        in_specs=[VMEM] * (at + POOL),
        out_specs=(VMEM,) * POOL,
        scratch_shapes=[pltpu.VMEM((key_count, 2 * HD), bf16)] * 2,
        input_output_aliases={at + j: j for j in range(POOL)},
        compiler_params=PARAMS,
        cost_estimate=cost(POOL * rows, key_count),
    )(*queries, *peaks, *pieces, *totals)


def refold(query, total, peak, blocks, every, semaphore):
    at = 0
    for piece in every:
        copy = pltpu.make_async_copy(piece, blocks.at[pl.ds(at, piece.shape[0])], semaphore)
        copy.start()
        copy.wait()
        at += piece.shape[0]
    total[...] = jnp.zeros_like(total)
    peak[...] = jnp.full(peak.shape, MASKED_SCORE, f32)
    rows = query.shape[0]
    ones = jnp.ones((BLOCK, HD), bf16)

    def step(b, _):
        key_rows = blocks[b, 0:BLOCK, :]
        scores = scored(query[...], jnp.concatenate([key_rows, key_rows], axis=1))
        old = peak[...]
        new = jnp.maximum(old, spread(jnp.max(scores, axis=1, keepdims=True), rows))
        weights = jnp.exp2(scores - new).astype(bf16)
        value_rows = jnp.concatenate([blocks[b, BLOCK : 2 * BLOCK, :], ones], axis=1)
        added = jnp.dot(weights, value_rows, preferred_element_type=f32)
        total[...] = total[...] * wide(jnp.exp2(old - new), 2 * HD) + added
        peak[...] = new
        return 0

    lax.fori_loop(0, at, step, 0)


def last_kernel(piece_count, every_count, *refs):
    query, peak_in, total_in, refs = refs[0], refs[1], refs[2], refs[3:]
    pieces, every, refs = refs[:piece_count], refs[piece_count:][:every_count], refs[piece_count + every_count :]
    out, total, peak, keys, values, blocks, semaphore = refs
    slots = out.shape[0]
    key_count = load_pieces(pieces, keys, values)
    total[...] = total_in[...]
    peak[...] = peak_in[...]
    for key_start in range(0, key_count, KEY_TILE):
        for start in range(0, query.shape[0], ROW_TILE):
            length = min(KEY_TILE, key_count - key_start)
            add_tile(query, total, peak, keys, values, pl.ds(start, ROW_TILE), key_start, length)

    @pl.when(jnp.logical_not(jnp.max(total[:, HD:]) < MASS_LIMIT))
    def _():
        refold(query, total, peak, blocks, every, semaphore)

    lane = lax.broadcasted_iota(jnp.int32, (slots, 128), 1)
    packed = jnp.zeros((slots, 128), f32)
    for h in range(H):
        rows = pl.ds(h * slots, slots)
        mass = total[rows, HD : 2 * HD]
        out[:, h * HD : (h + 1) * HD] = (total[rows, 0:HD] / mass).astype(bf16)
        level = peak[rows, :] + jnp.log2(mass)
        one = level.astype(bf16).astype(f32)
        two = (level - one).astype(bf16).astype(f32)
        three = level - one - two
        term = jnp.where(lane % 16 == 0, one, jnp.where(lane % 16 == 1, two, three))
        packed = jnp.where((lane // 16 == h) & (lane % 16 < 3), term, packed)
    out[:, H * HD :] = packed.astype(bf16)


def last_fold(query, peak, total, pieces, every):
    rows = query.shape[0]
    slots = rows // H
    key_count = sum(p.shape[0] for p in pieces) * BLOCK
    block_count = sum(p.shape[0] for p in every)
    return pl.pallas_call(
        lambda *refs: last_kernel(len(pieces), len(every), *refs),
        out_shape=jax.ShapeDtypeStruct((slots, H * HD + 128), bf16),
        in_specs=[VMEM] * (3 + len(pieces)) + [pl.BlockSpec(memory_space=pl.ANY)] * len(every),
        out_specs=VMEM,
        scratch_shapes=[
            pltpu.VMEM((rows, 2 * HD), f32),
            pltpu.VMEM((rows, HD), f32),
            pltpu.VMEM((key_count, 2 * HD), bf16),
            pltpu.VMEM((key_count, 2 * HD), bf16),
            pltpu.VMEM((block_count, 2 * BLOCK, HD), bf16),
            pltpu.SemaphoreType.DMA,
        ],
        compiler_params=PARAMS,
        cost_estimate=cost(rows, key_count),
    )(query, peak, total, *pieces, *every)


def combine_kernel(*refs):
    parts, suffix_quotient, suffix_level, request, out = refs[:-4], *refs[-4:]
    slots = out.shape[0]
    own = request_column(request[...], slots)[0]
    live = jnp.broadcast_to(own < slots, (slots, HD))
    lane = lax.broadcasted_iota(jnp.int32, (128, H * HD), 0)
    column = lax.broadcasted_iota(jnp.int32, (128, H * HD), 1)
    gather = ((lane // 16 == column // HD) & (lane % 16 < 3)).astype(bf16)
    levels = [
        jnp.dot(part[:, H * HD :], gather, preferred_element_type=f32) for part in parts
    ]
    for h in range(H):
        columns = slice(h * HD, (h + 1) * HD)
        rows = pl.ds(h * slots, slots)
        all_levels = [level[:, columns] for level in levels] + [suffix_level[rows, :]]
        all_quotients = [part[:, columns].astype(f32) for part in parts]
        all_quotients.append(suffix_quotient[rows, :])
        top = all_levels[0]
        for level in all_levels[1:]:
            top = jnp.maximum(top, level)
        upper = lower = 0.0
        for level, quotient in zip(all_levels, all_quotients):
            weight = jnp.exp2(level - top)
            upper = upper + weight * quotient
            lower = lower + weight
        out[:, columns] = jnp.where(live, upper / lower, 0.0).astype(bf16)


def combined(parts, suffix, request_row):
    slots = parts[0].shape[0]
    return pl.pallas_call(
        combine_kernel,
        out_shape=jax.ShapeDtypeStruct((slots, H * HD), bf16),
        in_specs=[VMEM] * (len(parts) + 3),
        out_specs=VMEM,
        compiler_params=PARAMS,
    )(*parts, *suffix, request_row)


def per_device(queries, suffix_keys, suffix_values, prefix_keys, prefix_values, slot_request):
    slots = queries.shape[0]
    request_row = slot_request.reshape(1, slots)
    own = jnp.concatenate([prefix_keys, prefix_values], axis=0)[None]

    far = [by_xor(own, dz=4), by_ring(own, dz=2), by_ring(own, dz=-2)]
    others = [
        by_xor(queries, dx=1, dz=1),
        by_xor(queries, dx=1),
        by_xor(queries, dz=1),
    ]
    first = jnp.concatenate([own, *far], axis=0)
    first, held_queries = lax.optimization_barrier((first, queries))
    query, *suffix = own_part(held_queries, suffix_keys, suffix_values, request_row)

    half_a, half_b = first[:2], first[2:]
    by_x = by_xor(first, dx=2)
    b_y = [by_ring(half_b, dy=1), by_ring(half_b, dy=-1), by_xor(half_b, dy=2)]
    by_x, *b_y = lax.optimization_barrier((by_x, *b_y))
    all_b_y = jnp.concatenate(b_y, axis=0)
    b_x = by_xor(all_b_y, dx=2)
    both_a = jnp.concatenate([half_a, by_x[:2]], axis=0)
    a_y = [by_ring(both_a, dy=1), by_ring(both_a, dy=-1), by_xor(both_a, dy=2)]
    pool, totals, peaks = first_fold(query, others, first)

    early = jnp.concatenate([first, by_x, all_b_y], axis=0)
    early, totals[0] = lax.optimization_barrier((early, totals[0]))
    early_c = by_xor(early, dc=1)
    totals = list(folded(pool, peaks, totals, [by_x, all_b_y]))
    totals = list(folded(pool, peaks, totals, [early_c]))
    *late, totals[0] = lax.optimization_barrier((*a_y, b_x, totals[0]))
    late_c = by_xor(jnp.concatenate(late, axis=0), dc=1)
    totals = list(folded(pool, peaks, totals, late))

    every = [first, by_x, all_b_y, early_c, *late, late_c]
    parts = []
    for j in (1, 2, 3, 0):
        parts.append(last_fold(pool[j], peaks[j], totals[j], [late_c], every))
    parts = [
        parts[3],
        by_xor(parts[0], dx=1, dz=1),
        by_xor(parts[1], dx=1),
        by_xor(parts[2], dz=1),
    ]
    return combined(parts, suffix, request_row)


def solution(mesh):
    placed = (
        P(AXES, None),
        P(AXES, None),
        P(AXES, None),
        P(AXES, None),
        P(AXES, None),
        P(AXES),
    )
    return jax.shard_map(
        per_device, mesh=mesh, in_specs=placed, out_specs=P(AXES, None), check_vma=False
    )
```

```python
import math

import jax
import jax.numpy as jnp
from jax import lax
from jax.experimental import pallas as pl
from jax.experimental.pallas import tpu as pltpu
from jax.sharding import PartitionSpec as P

H = 8
HD = 128
AXES = ("ctx", "req")
SCALE = 1.4426950408889634 / math.sqrt(HD)
MASKED_SCORE = -1e30
BLOCK = 128
POOL = 4
KEY_TILE = 512
ROW_TILE = 256
MASS_LIMIT = 2.0**100

f32, bf16 = jnp.float32, jnp.bfloat16
VMEM = pl.BlockSpec(memory_space=pltpu.VMEM)
PARAMS = pltpu.CompilerParams(vmem_limit_bytes=24 * 2**20)


def moved(array, place):
    pairs = []
    for x in range(4):
        for y in range(4):
            for z in range(8):
                for c in range(2):
                    pairs.append((linear(x, y, z, c), linear(*place(x, y, z, c))))
    return lax.ppermute(array, AXES, sorted(pairs))


def linear(x, y, z, c):
    return ((x % 2) * 4 + y) * 32 + (x // 2) * 16 + z * 2 + c


def by_xor(array, dx=0, dy=0, dz=0, dc=0):
    return moved(array, lambda x, y, z, c: (x ^ dx, y ^ dy, z ^ dz, c ^ dc))


def by_ring(array, dy=0, dz=0):
    return moved(array, lambda x, y, z, c: (x, (y + dy) % 4, (z + dz) % 8, c))


def wide(column_like, width):
    return jnp.concatenate([column_like] * (width // 128), axis=1)


def spread(column, rows):
    return jnp.broadcast_to(column, (rows, 128))


def prepare(source, out):
    slots = source.shape[0]
    for h in range(H):
        scaled = source[:, h * HD : (h + 1) * HD].astype(f32) * SCALE
        high = scaled.astype(bf16)
        low = (scaled - high.astype(f32)).astype(bf16)
        rows = pl.ds(h * slots, slots)
        out[rows, 0:HD] = high
        out[rows, HD : 2 * HD] = low


def scored(query, keys):
    return lax.dot_general(query, keys, (((1,), (1,)), ((), ())), preferred_element_type=f32)


def request_column(request_row, slots):
    row = lax.broadcasted_iota(jnp.int32, (slots, slots), 0)
    column = lax.broadcasted_iota(jnp.int32, (slots, slots), 1)
    across = jnp.broadcast_to(request_row, (slots, slots))
    return jnp.sum(jnp.where(row == column, across, 0), axis=1, keepdims=True), across, row, column


def cost(rows, keys):
    return pl.CostEstimate(
        flops=8 * rows * keys * HD, transcendentals=rows * keys, bytes_accessed=2048 * rows
    )


def own_kernel(*refs):
    sources, (query, quotient, level), held, semaphores = refs[:4], refs[4:7], refs[7:11], refs[11]
    copies = [pltpu.make_async_copy(a, b, semaphores.at[i]) for i, (a, b) in enumerate(zip(sources, held))]
    for copy in copies:
        copy.start()
    for copy in copies:
        copy.wait()
    queries, suffix_keys, suffix_values, request = held
    slots = queries.shape[0]
    prepare(queries, query)
    own, across, row, column = request_column(request[...], slots)
    visible = ((own == across) & (column <= row)).astype(jnp.int32)
    visible = jnp.concatenate([visible] * H, axis=0) == 1
    key_rows = jnp.concatenate([suffix_keys[...]] * 2, axis=1)
    scores = jnp.where(visible, scored(query[...], key_rows), MASKED_SCORE)
    peak = jnp.max(scores, axis=1, keepdims=True)
    weights = jnp.exp2(scores - peak).astype(bf16)
    value_rows = jnp.concatenate([suffix_values[...], jnp.ones((slots, HD), bf16)], axis=1)
    total = jnp.dot(weights, value_rows, preferred_element_type=f32)
    mass = total[:, HD:]
    quotient[...] = total[:, :HD] / mass
    level[...] = spread(peak, H * slots) + jnp.log2(mass)


def own_part(queries, suffix_keys, suffix_values, request_row):
    slots = queries.shape[0]
    shape = jax.ShapeDtypeStruct((H * slots, HD), f32)
    return pl.pallas_call(
        own_kernel,
        out_shape=(jax.ShapeDtypeStruct((H * slots, 2 * HD), bf16), shape, shape),
        in_specs=[pl.BlockSpec(memory_space=pl.ANY)] * 4,
        out_specs=(VMEM,) * 3,
        scratch_shapes=[
            pltpu.VMEM(a.shape, a.dtype) for a in (queries, suffix_keys, suffix_values, request_row)
        ]
        + [pltpu.SemaphoreType.DMA((4,))],
        compiler_params=PARAMS,
        cost_estimate=cost(H * slots, 512),
    )(queries, suffix_keys, suffix_values, request_row)


def load_pieces(pieces, keys, values):
    at = 0
    ones = jnp.ones((BLOCK, HD), bf16)
    for piece in pieces:
        for b in range(piece.shape[0]):
            rows = pl.ds(at, BLOCK)
            key_rows = piece[b, 0:BLOCK, :]
            keys[rows, 0:HD] = key_rows
            keys[rows, HD : 2 * HD] = key_rows
            values[rows, 0:HD] = piece[b, BLOCK : 2 * BLOCK, :]
            values[rows, HD : 2 * HD] = ones
            at += BLOCK
    return at


def first_kernel(*refs):
    query, refs = refs[0], refs[1:]
    others, piece, refs = refs[: POOL - 1], refs[POOL - 1], refs[POOL:]
    prepared, totals, peaks = refs[: POOL - 1], refs[POOL - 1 : 2 * POOL - 1], refs[2 * POOL - 1 : 3 * POOL - 1]
    keys, values = refs[3 * POOL - 1 :]
    key_count = load_pieces([piece], keys, values)
    for source, out in zip(others, prepared):
        prepare(source, out)
    for j, held in enumerate([query, *prepared]):
        for start in range(0, held.shape[0], ROW_TILE):
            rows = pl.ds(start, ROW_TILE)
            scores = scored(held[rows, :], keys[...])
            peak = spread(jnp.max(scores, axis=1, keepdims=True), ROW_TILE)
            weights = jnp.exp2(scores - wide(peak, key_count)).astype(bf16)
            totals[j][rows, :] = jnp.dot(weights, values[...], preferred_element_type=f32)
            peaks[j][rows, :] = peak


def first_fold(query, others, piece):
    rows, key_count = query.shape[0], piece.shape[0] * BLOCK
    shapes = (
        [jax.ShapeDtypeStruct((rows, 2 * HD), bf16)] * (POOL - 1)
        + [jax.ShapeDtypeStruct((rows, 2 * HD), f32)] * POOL
        + [jax.ShapeDtypeStruct((rows, HD), f32)] * POOL
    )
    outs = pl.pallas_call(
        first_kernel,
        out_shape=tuple(shapes),
        in_specs=[VMEM] * (POOL + 1),
        out_specs=(VMEM,) * len(shapes),
        scratch_shapes=[pltpu.VMEM((key_count, 2 * HD), bf16)] * 2,
        compiler_params=PARAMS,
        cost_estimate=cost(POOL * rows, key_count + 512),
    )(query, *others, piece)
    return [query, *outs[: POOL - 1]], list(outs[POOL - 1 : 2 * POOL - 1]), outs[2 * POOL - 1 :]


def add_tile(query, held, total, peak, keys, values, rows, start, length):
    span = pl.ds(start, length)
    weights = jnp.exp2(scored(query[rows, :], keys[span, :]) - wide(peak[rows, :], length))
    added = jnp.dot(weights.astype(bf16), values[span, :], preferred_element_type=f32)
    total[rows, :] = held[rows, :] + added


def fold_kernel(count, piece_count, *refs):
    queries, peaks, refs = refs[:count], refs[count : 2 * count], refs[2 * count :]
    pieces, refs = refs[:piece_count], refs[piece_count:]
    totals, (keys, values) = refs[count : 2 * count], refs[2 * count :]
    key_count = load_pieces(pieces, keys, values)
    for key_start in range(0, key_count, KEY_TILE):
        length = min(KEY_TILE, key_count - key_start)
        for j in range(count):
            for start in range(0, queries[j].shape[0], ROW_TILE):
                rows = pl.ds(start, ROW_TILE)
                held = refs[j] if key_start == 0 else totals[j]
                add_tile(queries[j], held, totals[j], peaks[j], keys, values, rows, key_start, length)


def folded(queries, peaks, totals, pieces):
    rows, count = queries[0].shape[0], len(queries)
    key_count = sum(p.shape[0] for p in pieces) * BLOCK
    at = 2 * count + len(pieces)
    return pl.pallas_call(
        lambda *refs: fold_kernel(count, len(pieces), *refs),
        out_shape=(jax.ShapeDtypeStruct((rows, 2 * HD), f32),) * count,
        in_specs=[VMEM] * (at + count),
        out_specs=(VMEM,) * count,
        scratch_shapes=[pltpu.VMEM((key_count, 2 * HD), bf16)] * 2,
        input_output_aliases={at + j: j for j in range(count)},
        compiler_params=PARAMS,
        cost_estimate=cost(count * rows, key_count),
    )(*queries, *peaks, *pieces, *totals)


def refold(query, total, peak, blocks, every, semaphore):
    at = 0
    for piece in every:
        copy = pltpu.make_async_copy(piece, blocks.at[pl.ds(at, piece.shape[0])], semaphore)
        copy.start()
        copy.wait()
        at += piece.shape[0]
    total[...] = jnp.zeros_like(total)
    peak[...] = jnp.full(peak.shape, MASKED_SCORE, f32)
    rows = query.shape[0]
    ones = jnp.ones((BLOCK, HD), bf16)

    def step(b, _):
        key_rows = blocks[b, 0:BLOCK, :]
        scores = scored(query[...], jnp.concatenate([key_rows, key_rows], axis=1))
        old = peak[...]
        new = jnp.maximum(old, spread(jnp.max(scores, axis=1, keepdims=True), rows))
        weights = jnp.exp2(scores - new).astype(bf16)
        value_rows = jnp.concatenate([blocks[b, BLOCK : 2 * BLOCK, :], ones], axis=1)
        added = jnp.dot(weights, value_rows, preferred_element_type=f32)
        total[...] = total[...] * wide(jnp.exp2(old - new), 2 * HD) + added
        peak[...] = new
        return 0

    lax.fori_loop(0, at, step, 0)


def last_kernel(piece_count, every_count, *refs):
    query, peak_in, total_in, refs = refs[0], refs[1], refs[2], refs[3:]
    pieces, every, refs = refs[:piece_count], refs[piece_count:][:every_count], refs[piece_count + every_count :]
    out, total, peak, keys, values, blocks, semaphore = refs
    slots = out.shape[0]
    key_count = load_pieces(pieces, keys, values)
    peak[...] = peak_in[...]
    for key_start in range(0, key_count, KEY_TILE):
        for start in range(0, query.shape[0], ROW_TILE):
            length = min(KEY_TILE, key_count - key_start)
            held = total_in if key_start == 0 else total
            add_tile(query, held, total, peak_in, keys, values, pl.ds(start, ROW_TILE), key_start, length)

    @pl.when(jnp.logical_not(jnp.max(total[:, HD:]) < MASS_LIMIT))
    def _():
        refold(query, total, peak, blocks, every, semaphore)

    lane = lax.broadcasted_iota(jnp.int32, (slots, 128), 1)
    packed = jnp.zeros((slots, 128), f32)
    for h in range(H):
        rows = pl.ds(h * slots, slots)
        mass = total[rows, HD : 2 * HD]
        out[:, h * HD : (h + 1) * HD] = (total[rows, 0:HD] / mass).astype(bf16)
        level = peak[rows, :] + jnp.log2(mass)
        one = level.astype(bf16).astype(f32)
        two = (level - one).astype(bf16).astype(f32)
        three = level - one - two
        term = jnp.where(lane % 16 == 0, one, jnp.where(lane % 16 == 1, two, three))
        packed = jnp.where((lane // 16 == h) & (lane % 16 < 3), term, packed)
    out[:, H * HD :] = packed.astype(bf16)


def last_fold(query, peak, total, pieces, every):
    rows = query.shape[0]
    slots = rows // H
    key_count = sum(p.shape[0] for p in pieces) * BLOCK
    block_count = sum(p.shape[0] for p in every)
    return pl.pallas_call(
        lambda *refs: last_kernel(len(pieces), len(every), *refs),
        out_shape=jax.ShapeDtypeStruct((slots, H * HD + 128), bf16),
        in_specs=[VMEM] * (3 + len(pieces)) + [pl.BlockSpec(memory_space=pl.ANY)] * len(every),
        out_specs=VMEM,
        scratch_shapes=[
            pltpu.VMEM((rows, 2 * HD), f32),
            pltpu.VMEM((rows, HD), f32),
            pltpu.VMEM((key_count, 2 * HD), bf16),
            pltpu.VMEM((key_count, 2 * HD), bf16),
            pltpu.VMEM((block_count, 2 * BLOCK, HD), bf16),
            pltpu.SemaphoreType.DMA,
        ],
        compiler_params=PARAMS,
        cost_estimate=cost(rows, key_count),
    )(query, peak, total, *pieces, *every)


def combine_kernel(*refs):
    parts, suffix_quotient, suffix_level, request, out = refs[:-4], *refs[-4:]
    slots = out.shape[0]
    own = request_column(request[...], slots)[0]
    live = jnp.broadcast_to(own < slots, (slots, HD))
    lane = lax.broadcasted_iota(jnp.int32, (128, H * HD), 0)
    column = lax.broadcasted_iota(jnp.int32, (128, H * HD), 1)
    gather = ((lane // 16 == column // HD) & (lane % 16 < 3)).astype(bf16)
    levels = [
        jnp.dot(part[:, H * HD :], gather, preferred_element_type=f32) for part in parts
    ]
    for h in range(H):
        columns = slice(h * HD, (h + 1) * HD)
        rows = pl.ds(h * slots, slots)
        all_levels = [level[:, columns] for level in levels] + [suffix_level[rows, :]]
        all_quotients = [part[:, columns].astype(f32) for part in parts]
        all_quotients.append(suffix_quotient[rows, :])
        top = all_levels[0]
        for level in all_levels[1:]:
            top = jnp.maximum(top, level)
        upper = lower = 0.0
        for level, quotient in zip(all_levels, all_quotients):
            weight = jnp.exp2(level - top)
            upper = upper + weight * quotient
            lower = lower + weight
        out[:, columns] = jnp.where(live, upper / lower, 0.0).astype(bf16)


def combined(parts, suffix, request_row):
    slots = parts[0].shape[0]
    return pl.pallas_call(
        combine_kernel,
        out_shape=jax.ShapeDtypeStruct((slots, H * HD), bf16),
        in_specs=[VMEM] * (len(parts) + 3),
        out_specs=VMEM,
        compiler_params=PARAMS,
    )(*parts, *suffix, request_row)


def per_device(queries, suffix_keys, suffix_values, prefix_keys, prefix_values, slot_request):
    slots = queries.shape[0]
    request_row = slot_request.reshape(1, slots)
    own = jnp.concatenate([prefix_keys, prefix_values], axis=0)[None]

    far = [by_xor(own, dz=4), by_ring(own, dz=2), by_ring(own, dz=-2)]
    others = [
        by_xor(queries, dx=1, dz=1),
        by_xor(queries, dx=1),
        by_xor(queries, dz=1),
    ]
    first = jnp.concatenate([own, *far], axis=0)
    first, held_queries = lax.optimization_barrier((first, queries))
    query, *suffix = own_part(held_queries, suffix_keys, suffix_values, request_row)

    half_a, half_b = first[:2], first[2:]
    by_x = by_xor(first, dx=2)
    b_y = [by_ring(half_b, dy=1), by_ring(half_b, dy=-1), by_xor(half_b, dy=2)]
    by_x, *b_y = lax.optimization_barrier((by_x, *b_y))
    all_b_y = jnp.concatenate(b_y, axis=0)
    b_x = by_xor(all_b_y, dx=2)
    both_a = jnp.concatenate([half_a, by_x[:2]], axis=0)
    a_y = [by_ring(both_a, dy=1), by_ring(both_a, dy=-1), by_xor(both_a, dy=2)]
    pool, totals, peaks = first_fold(query, others, first)

    early = jnp.concatenate([first, by_x, all_b_y], axis=0)
    early, totals[0] = lax.optimization_barrier((early, totals[0]))
    early_c = by_xor(early, dc=1)
    totals = list(folded(pool, peaks, totals, [by_x, all_b_y]))
    totals = list(folded(pool, peaks, totals, [early_c]))
    *late, totals[0] = lax.optimization_barrier((*a_y, b_x, totals[0]))
    late_c = by_xor(jnp.concatenate(late, axis=0), dc=1)
    totals[1:] = folded(pool[1:], peaks[1:], totals[1:], late)

    every = [first, by_x, all_b_y, early_c, *late, late_c]
    parts = []
    for j in (1, 2, 3, 0):
        pieces = [late_c] if j else [*late, late_c]
        parts.append(last_fold(pool[j], peaks[j], totals[j], pieces, every))
    parts = [
        parts[3],
        by_xor(parts[0], dx=1, dz=1),
        by_xor(parts[1], dx=1),
        by_xor(parts[2], dz=1),
    ]
    return combined(parts, suffix, request_row)


def solution(mesh):
    placed = (
        P(AXES, None),
        P(AXES, None),
        P(AXES, None),
        P(AXES, None),
        P(AXES, None),
        P(AXES),
    )
    return jax.shard_map(
        per_device, mesh=mesh, in_specs=placed, out_specs=P(AXES, None), check_vma=False
    )
```

```python
import math

import jax
import jax.numpy as jnp
from jax import lax
from jax.experimental import pallas as pl
from jax.experimental.pallas import tpu as pltpu
from jax.sharding import PartitionSpec as P

H = 8
HD = 128
AXES = ("ctx", "req")
SCALE = 1.4426950408889634 / math.sqrt(HD)
MASKED_SCORE = -1e30
BLOCK = 128
POOL = 4
KEY_TILE = 512
ROW_TILE = 256
MASS_LIMIT = 2.0**100

f32, bf16 = jnp.float32, jnp.bfloat16
VMEM = pl.BlockSpec(memory_space=pltpu.VMEM)
PARAMS = pltpu.CompilerParams(vmem_limit_bytes=24 * 2**20)


def moved(array, place):
    pairs = []
    for x in range(4):
        for y in range(4):
            for z in range(8):
                for c in range(2):
                    pairs.append((linear(x, y, z, c), linear(*place(x, y, z, c))))
    return lax.ppermute(array, AXES, sorted(pairs))


def linear(x, y, z, c):
    return ((x % 2) * 4 + y) * 32 + (x // 2) * 16 + z * 2 + c


def by_xor(array, dx=0, dy=0, dz=0, dc=0):
    return moved(array, lambda x, y, z, c: (x ^ dx, y ^ dy, z ^ dz, c ^ dc))


def by_ring(array, dy=0, dz=0):
    return moved(array, lambda x, y, z, c: (x, (y + dy) % 4, (z + dz) % 8, c))


def wide(column_like, width):
    return jnp.concatenate([column_like] * (width // 128), axis=1)


def spread(column, rows):
    return jnp.broadcast_to(column, (rows, 128))


def prepare(source, out):
    slots = source.shape[0]
    for h in range(H):
        scaled = source[:, h * HD : (h + 1) * HD].astype(f32) * SCALE
        high = scaled.astype(bf16)
        low = (scaled - high.astype(f32)).astype(bf16)
        rows = pl.ds(h * slots, slots)
        out[rows, 0:HD] = high
        out[rows, HD : 2 * HD] = low


def scored(query, keys):
    return lax.dot_general(query, keys, (((1,), (1,)), ((), ())), preferred_element_type=f32)


def request_column(request_row, slots):
    row = lax.broadcasted_iota(jnp.int32, (slots, slots), 0)
    column = lax.broadcasted_iota(jnp.int32, (slots, slots), 1)
    across = jnp.broadcast_to(request_row, (slots, slots))
    return jnp.sum(jnp.where(row == column, across, 0), axis=1, keepdims=True), across, row, column


def cost(rows, keys):
    return pl.CostEstimate(
        flops=8 * rows * keys * HD, transcendentals=rows * keys, bytes_accessed=2048 * rows
    )


def own_kernel(*refs):
    sources, (query, quotient, level), held, semaphores = refs[:4], refs[4:7], refs[7:11], refs[11]
    copies = [pltpu.make_async_copy(a, b, semaphores.at[i]) for i, (a, b) in enumerate(zip(sources, held))]
    for copy in copies:
        copy.start()
    for copy in copies:
        copy.wait()
    queries, suffix_keys, suffix_values, request = held
    slots = queries.shape[0]
    prepare(queries, query)
    own, across, row, column = request_column(request[...], slots)
    visible = ((own == across) & (column <= row)).astype(jnp.int32)
    visible = jnp.concatenate([visible] * H, axis=0) == 1
    key_rows = jnp.concatenate([suffix_keys[...]] * 2, axis=1)
    scores = jnp.where(visible, scored(query[...], key_rows), MASKED_SCORE)
    peak = jnp.max(scores, axis=1, keepdims=True)
    weights = jnp.exp2(scores - peak).astype(bf16)
    value_rows = jnp.concatenate([suffix_values[...], jnp.ones((slots, HD), bf16)], axis=1)
    total = jnp.dot(weights, value_rows, preferred_element_type=f32)
    mass = total[:, HD:]
    quotient[...] = total[:, :HD] / mass
    level[...] = spread(peak, H * slots) + jnp.log2(mass)


def own_part(queries, suffix_keys, suffix_values, request_row):
    slots = queries.shape[0]
    shape = jax.ShapeDtypeStruct((H * slots, HD), f32)
    return pl.pallas_call(
        own_kernel,
        out_shape=(jax.ShapeDtypeStruct((H * slots, 2 * HD), bf16), shape, shape),
        in_specs=[pl.BlockSpec(memory_space=pl.ANY)] * 4,
        out_specs=(VMEM,) * 3,
        scratch_shapes=[
            pltpu.VMEM(a.shape, a.dtype) for a in (queries, suffix_keys, suffix_values, request_row)
        ]
        + [pltpu.SemaphoreType.DMA((4,))],
        compiler_params=PARAMS,
        cost_estimate=cost(H * slots, 512),
    )(queries, suffix_keys, suffix_values, request_row)


def load_pieces(pieces, keys, values):
    at = 0
    ones = jnp.ones((BLOCK, HD), bf16)
    for piece in pieces:
        for b in range(piece.shape[0]):
            rows = pl.ds(at, BLOCK)
            key_rows = piece[b, 0:BLOCK, :]
            keys[rows, 0:HD] = key_rows
            keys[rows, HD : 2 * HD] = key_rows
            values[rows, 0:HD] = piece[b, BLOCK : 2 * BLOCK, :]
            values[rows, HD : 2 * HD] = ones
            at += BLOCK
    return at


def first_kernel(*refs):
    query, refs = refs[0], refs[1:]
    others, piece, refs = refs[: POOL - 1], refs[POOL - 1], refs[POOL:]
    prepared, totals, peaks = refs[: POOL - 1], refs[POOL - 1 : 2 * POOL - 1], refs[2 * POOL - 1 : 3 * POOL - 1]
    keys, values = refs[3 * POOL - 1 :]
    key_count = load_pieces([piece], keys, values)
    for source, out in zip(others, prepared):
        prepare(source, out)
    for j, held in enumerate([query, *prepared]):
        for start in range(0, held.shape[0], ROW_TILE):
            rows = pl.ds(start, ROW_TILE)
            scores = scored(held[rows, :], keys[...])
            peak = spread(jnp.max(scores, axis=1, keepdims=True), ROW_TILE)
            weights = jnp.exp2(scores - wide(peak, key_count)).astype(bf16)
            totals[j][rows, :] = jnp.dot(weights, values[...], preferred_element_type=f32)
            peaks[j][rows, :] = peak


def first_fold(query, others, piece):
    rows, key_count = query.shape[0], piece.shape[0] * BLOCK
    shapes = (
        [jax.ShapeDtypeStruct((rows, 2 * HD), bf16)] * (POOL - 1)
        + [jax.ShapeDtypeStruct((rows, 2 * HD), f32)] * POOL
        + [jax.ShapeDtypeStruct((rows, HD), f32)] * POOL
    )
    outs = pl.pallas_call(
        first_kernel,
        out_shape=tuple(shapes),
        in_specs=[VMEM] * (POOL + 1),
        out_specs=(VMEM,) * len(shapes),
        scratch_shapes=[pltpu.VMEM((key_count, 2 * HD), bf16)] * 2,
        compiler_params=PARAMS,
        cost_estimate=cost(POOL * rows, key_count + 512),
    )(query, *others, piece)
    return [query, *outs[: POOL - 1]], list(outs[POOL - 1 : 2 * POOL - 1]), outs[2 * POOL - 1 :]


def add_tile(query, held, total, peak, keys, values, rows, start, length):
    span = pl.ds(start, length)
    weights = jnp.exp2(scored(query[rows, :], keys[span, :]) - wide(peak[rows, :], length))
    added = jnp.dot(weights.astype(bf16), values[span, :], preferred_element_type=f32)
    total[rows, :] = held[rows, :] + added


def fold_kernel(count, piece_count, looped, *refs):
    queries, peaks, refs = refs[:count], refs[count : 2 * count], refs[2 * count :]
    pieces, refs = refs[:piece_count], refs[piece_count:]
    totals, (keys, values) = refs[count : 2 * count], refs[2 * count :]
    key_count = load_pieces(pieces, keys, values)

    def add_all(held, key_start, length):
        for j in range(count):
            for start in range(0, queries[j].shape[0], ROW_TILE):
                rows = pl.ds(start, ROW_TILE)
                add_tile(queries[j], held[j], totals[j], peaks[j], keys, values, rows, key_start, length)

    def step(i, _):
        add_all(totals, pl.multiple_of(i * KEY_TILE, KEY_TILE), KEY_TILE)
        return 0

    if looped:
        for held, total in zip(refs[:count], totals):
            total[...] = held[...]
        lax.fori_loop(0, key_count // KEY_TILE, step, 0)
        rest = key_count % KEY_TILE
        if rest:
            add_all(totals, key_count - rest, rest)
    else:
        for key_start in range(0, key_count, KEY_TILE):
            length = min(KEY_TILE, key_count - key_start)
            add_all(totals if key_start else refs[:count], key_start, length)


def folded(queries, peaks, totals, pieces, looped=False):
    rows, count = queries[0].shape[0], len(queries)
    key_count = sum(p.shape[0] for p in pieces) * BLOCK
    at = 2 * count + len(pieces)
    return pl.pallas_call(
        lambda *refs: fold_kernel(count, len(pieces), looped, *refs),
        out_shape=(jax.ShapeDtypeStruct((rows, 2 * HD), f32),) * count,
        in_specs=[VMEM] * (at + count),
        out_specs=(VMEM,) * count,
        scratch_shapes=[pltpu.VMEM((key_count, 2 * HD), bf16)] * 2,
        input_output_aliases={at + j: j for j in range(count)},
        compiler_params=PARAMS,
        cost_estimate=cost(count * rows, key_count),
    )(*queries, *peaks, *pieces, *totals)


def refold(query, total, peak, blocks, every, semaphore):
    at = 0
    for piece in every:
        copy = pltpu.make_async_copy(piece, blocks.at[pl.ds(at, piece.shape[0])], semaphore)
        copy.start()
        copy.wait()
        at += piece.shape[0]
    total[...] = jnp.zeros_like(total)
    peak[...] = jnp.full(peak.shape, MASKED_SCORE, f32)
    ones = jnp.ones((BLOCK, HD), bf16)

    def step(i, _):
        b = i // (query.shape[0] // 64)
        rows = pl.ds(pl.multiple_of(i % (query.shape[0] // 64) * 64, 64), 64)
        key_rows = blocks[b, 0:BLOCK, :]
        scores = scored(query[rows, :], jnp.concatenate([key_rows, key_rows], axis=1))
        old = peak[rows, :]
        new = jnp.maximum(old, spread(jnp.max(scores, axis=1, keepdims=True), 64))
        weights = jnp.exp2(scores - new).astype(bf16)
        value_rows = jnp.concatenate([blocks[b, BLOCK : 2 * BLOCK, :], ones], axis=1)
        added = jnp.dot(weights, value_rows, preferred_element_type=f32)
        total[rows, :] = total[rows, :] * wide(jnp.exp2(old - new), 2 * HD) + added
        peak[rows, :] = new
        return 0

    lax.fori_loop(0, at * (query.shape[0] // 64), step, 0)


def last_kernel(piece_count, every_count, *refs):
    query, peak_in, total_in, refs = refs[0], refs[1], refs[2], refs[3:]
    pieces, every, refs = refs[:piece_count], refs[piece_count:][:every_count], refs[piece_count + every_count :]
    out, total, peak, keys, values, blocks, semaphore = refs
    slots = out.shape[0]
    key_count = load_pieces(pieces, keys, values)
    peak[...] = peak_in[...]
    for key_start in range(0, key_count, KEY_TILE):
        for start in range(0, query.shape[0], ROW_TILE):
            length = min(KEY_TILE, key_count - key_start)
            held = total_in if key_start == 0 else total
            add_tile(query, held, total, peak_in, keys, values, pl.ds(start, ROW_TILE), key_start, length)

    @pl.when(jnp.logical_not(jnp.max(total[:, HD:]) < MASS_LIMIT))
    def _():
        refold(query, total, peak, blocks, every, semaphore)

    lane = lax.broadcasted_iota(jnp.int32, (slots, 128), 1)
    packed = jnp.zeros((slots, 128), f32)
    for h in range(H):
        rows = pl.ds(h * slots, slots)
        mass = total[rows, HD : 2 * HD]
        out[:, h * HD : (h + 1) * HD] = (total[rows, 0:HD] / mass).astype(bf16)
        level = peak[rows, :] + jnp.log2(mass)
        one = level.astype(bf16).astype(f32)
        two = (level - one).astype(bf16).astype(f32)
        three = level - one - two
        term = jnp.where(lane % 16 == 0, one, jnp.where(lane % 16 == 1, two, three))
        packed = jnp.where((lane // 16 == h) & (lane % 16 < 3), term, packed)
    out[:, H * HD :] = packed.astype(bf16)


def last_fold(query, peak, total, pieces, every):
    rows = query.shape[0]
    slots = rows // H
    key_count = sum(p.shape[0] for p in pieces) * BLOCK
    block_count = sum(p.shape[0] for p in every)
    return pl.pallas_call(
        lambda *refs: last_kernel(len(pieces), len(every), *refs),
        out_shape=jax.ShapeDtypeStruct((slots, H * HD + 128), bf16),
        in_specs=[VMEM] * (3 + len(pieces)) + [pl.BlockSpec(memory_space=pl.ANY)] * len(every),
        out_specs=VMEM,
        scratch_shapes=[
            pltpu.VMEM((rows, 2 * HD), f32),
            pltpu.VMEM((rows, HD), f32),
            pltpu.VMEM((key_count, 2 * HD), bf16),
            pltpu.VMEM((key_count, 2 * HD), bf16),
            pltpu.VMEM((block_count, 2 * BLOCK, HD), bf16),
            pltpu.SemaphoreType.DMA,
        ],
        compiler_params=PARAMS,
        cost_estimate=cost(rows, key_count),
    )(query, peak, total, *pieces, *every)


def combine_kernel(*refs):
    parts, suffix_quotient, suffix_level, request, out = refs[:-4], *refs[-4:]
    slots = out.shape[0]
    own = request_column(request[...], slots)[0]
    live = jnp.broadcast_to(own < slots, (slots, HD))
    lane = lax.broadcasted_iota(jnp.int32, (128, H * HD), 0)
    column = lax.broadcasted_iota(jnp.int32, (128, H * HD), 1)
    gather = ((lane // 16 == column // HD) & (lane % 16 < 3)).astype(bf16)
    levels = [
        jnp.dot(part[:, H * HD :], gather, preferred_element_type=f32) for part in parts
    ]
    for h in range(H):
        columns = slice(h * HD, (h + 1) * HD)
        rows = pl.ds(h * slots, slots)
        all_levels = [level[:, columns] for level in levels] + [suffix_level[rows, :]]
        all_quotients = [part[:, columns].astype(f32) for part in parts]
        all_quotients.append(suffix_quotient[rows, :])
        top = all_levels[0]
        for level in all_levels[1:]:
            top = jnp.maximum(top, level)
        upper = lower = 0.0
        for level, quotient in zip(all_levels, all_quotients):
            weight = jnp.exp2(level - top)
            upper = upper + weight * quotient
            lower = lower + weight
        out[:, columns] = jnp.where(live, upper / lower, 0.0).astype(bf16)


def combined(parts, suffix, request_row):
    slots = parts[0].shape[0]
    return pl.pallas_call(
        combine_kernel,
        out_shape=jax.ShapeDtypeStruct((slots, H * HD), bf16),
        in_specs=[VMEM] * (len(parts) + 3),
        out_specs=VMEM,
        compiler_params=PARAMS,
    )(*parts, *suffix, request_row)


def per_device(queries, suffix_keys, suffix_values, prefix_keys, prefix_values, slot_request):
    slots = queries.shape[0]
    request_row = slot_request.reshape(1, slots)
    own = jnp.concatenate([prefix_keys, prefix_values], axis=0)[None]

    far = [by_xor(own, dz=4), by_ring(own, dz=2), by_ring(own, dz=-2)]
    others = [
        by_xor(queries, dx=1, dz=1),
        by_xor(queries, dx=1),
        by_xor(queries, dz=1),
    ]
    first = jnp.concatenate([own, *far], axis=0)
    first, held_queries = lax.optimization_barrier((first, queries))
    query, *suffix = own_part(held_queries, suffix_keys, suffix_values, request_row)

    half_a, half_b = first[:2], first[2:]
    by_x = by_xor(first, dx=2)
    b_y = [by_ring(half_b, dy=1), by_ring(half_b, dy=-1), by_xor(half_b, dy=2)]
    by_x, *b_y = lax.optimization_barrier((by_x, *b_y))
    all_b_y = jnp.concatenate(b_y, axis=0)
    b_x = by_xor(all_b_y, dx=2)
    both_a = jnp.concatenate([half_a, by_x[:2]], axis=0)
    a_y = [by_ring(both_a, dy=1), by_ring(both_a, dy=-1), by_xor(both_a, dy=2)]
    pool, totals, peaks = first_fold(query, others, first)

    early = jnp.concatenate([first, by_x, all_b_y], axis=0)
    early, totals[0] = lax.optimization_barrier((early, totals[0]))
    early_c = by_xor(early, dc=1)
    totals = list(folded(pool, peaks, totals, [by_x, all_b_y], looped=True))
    totals = list(folded(pool, peaks, totals, [early_c], looped=True))
    *late, totals[0] = lax.optimization_barrier((*a_y, b_x, totals[0]))
    late_c = by_xor(jnp.concatenate(late, axis=0), dc=1)
    totals[1:] = folded(pool[1:], peaks[1:], totals[1:], late)

    every = [first, by_x, all_b_y, early_c, *late, late_c]
    parts = []
    for j in (1, 2, 3, 0):
        pieces = [late_c] if j else [*late, late_c]
        parts.append(last_fold(pool[j], peaks[j], totals[j], pieces, every))
    parts = [
        parts[3],
        by_xor(parts[0], dx=1, dz=1),
        by_xor(parts[1], dx=1),
        by_xor(parts[2], dz=1),
    ]
    return combined(parts, suffix, request_row)


def solution(mesh):
    placed = (
        P(AXES, None),
        P(AXES, None),
        P(AXES, None),
        P(AXES, None),
        P(AXES, None),
        P(AXES),
    )
    return jax.shard_map(
        per_device, mesh=mesh, in_specs=placed, out_specs=P(AXES, None), check_vma=False
    )
```

```python
import math

import jax
import jax.numpy as jnp
from jax import lax
from jax.experimental import pallas as pl
from jax.experimental.pallas import tpu as pltpu
from jax.sharding import PartitionSpec as P

H = 8
HD = 128
AXES = ("ctx", "req")
SCALE = 1.4426950408889634 / math.sqrt(HD)
MASKED_SCORE = -1e30
BLOCK = 128
POOL = 4
KEY_TILE = 512
ROW_TILE = 256
MASS_LIMIT = 2.0**100

f32, bf16 = jnp.float32, jnp.bfloat16
VMEM = pl.BlockSpec(memory_space=pltpu.VMEM)
PARAMS = pltpu.CompilerParams(vmem_limit_bytes=24 * 2**20)


def moved(array, place):
    pairs = []
    for x in range(4):
        for y in range(4):
            for z in range(8):
                for c in range(2):
                    pairs.append((linear(x, y, z, c), linear(*place(x, y, z, c))))
    return lax.ppermute(array, AXES, sorted(pairs))


def linear(x, y, z, c):
    return ((x % 2) * 4 + y) * 32 + (x // 2) * 16 + z * 2 + c


def by_xor(array, dx=0, dy=0, dz=0, dc=0):
    return moved(array, lambda x, y, z, c: (x ^ dx, y ^ dy, z ^ dz, c ^ dc))


def by_ring(array, dy=0, dz=0):
    return moved(array, lambda x, y, z, c: (x, (y + dy) % 4, (z + dz) % 8, c))


def wide(column_like, width):
    return jnp.concatenate([column_like] * (width // 128), axis=1)


def spread(column, rows):
    return jnp.broadcast_to(column, (rows, 128))


def prepare(source, out):
    slots = source.shape[0]
    for h in range(H):
        scaled = source[:, h * HD : (h + 1) * HD].astype(f32) * SCALE
        high = scaled.astype(bf16)
        low = (scaled - high.astype(f32)).astype(bf16)
        rows = pl.ds(h * slots, slots)
        out[rows, 0:HD] = high
        out[rows, HD : 2 * HD] = low


def scored(query, keys):
    return lax.dot_general(query, keys, (((1,), (1,)), ((), ())), preferred_element_type=f32)


def request_column(request_row, slots):
    row = lax.broadcasted_iota(jnp.int32, (slots, slots), 0)
    column = lax.broadcasted_iota(jnp.int32, (slots, slots), 1)
    across = jnp.broadcast_to(request_row, (slots, slots))
    return jnp.sum(jnp.where(row == column, across, 0), axis=1, keepdims=True), across, row, column


def cost(rows, keys):
    return pl.CostEstimate(
        flops=8 * rows * keys * HD, transcendentals=rows * keys, bytes_accessed=2048 * rows
    )


def own_kernel(*refs):
    sources, (query, quotient, level), held, semaphores = refs[:4], refs[4:7], refs[7:11], refs[11]
    copies = [pltpu.make_async_copy(a, b, semaphores.at[i]) for i, (a, b) in enumerate(zip(sources, held))]
    for copy in copies:
        copy.start()
    for copy in copies:
        copy.wait()
    queries, suffix_keys, suffix_values, request = held
    slots = queries.shape[0]
    prepare(queries, query)
    own, across, row, column = request_column(request[...], slots)
    visible = ((own == across) & (column <= row)).astype(jnp.int32)
    visible = jnp.concatenate([visible] * H, axis=0) == 1
    key_rows = jnp.concatenate([suffix_keys[...]] * 2, axis=1)
    scores = jnp.where(visible, scored(query[...], key_rows), MASKED_SCORE)
    peak = jnp.max(scores, axis=1, keepdims=True)
    weights = jnp.exp2(scores - peak).astype(bf16)
    value_rows = jnp.concatenate([suffix_values[...], jnp.ones((slots, HD), bf16)], axis=1)
    total = jnp.dot(weights, value_rows, preferred_element_type=f32)
    mass = total[:, HD:]
    quotient[...] = total[:, :HD] / mass
    level[...] = spread(peak, H * slots) + jnp.log2(mass)


def own_part(queries, suffix_keys, suffix_values, request_row):
    slots = queries.shape[0]
    shape = jax.ShapeDtypeStruct((H * slots, HD), f32)
    return pl.pallas_call(
        own_kernel,
        out_shape=(jax.ShapeDtypeStruct((H * slots, 2 * HD), bf16), shape, shape),
        in_specs=[pl.BlockSpec(memory_space=pl.ANY)] * 4,
        out_specs=(VMEM,) * 3,
        scratch_shapes=[
            pltpu.VMEM(a.shape, a.dtype) for a in (queries, suffix_keys, suffix_values, request_row)
        ]
        + [pltpu.SemaphoreType.DMA((4,))],
        compiler_params=PARAMS,
        cost_estimate=cost(H * slots, 512),
    )(queries, suffix_keys, suffix_values, request_row)


def load_pieces(pieces, keys, values):
    at = 0
    ones = jnp.ones((BLOCK, HD), bf16)
    for piece in pieces:
        for b in range(piece.shape[0]):
            rows = pl.ds(at, BLOCK)
            key_rows = piece[b, 0:BLOCK, :]
            keys[rows, 0:HD] = key_rows
            keys[rows, HD : 2 * HD] = key_rows
            values[rows, 0:HD] = piece[b, BLOCK : 2 * BLOCK, :]
            values[rows, HD : 2 * HD] = ones
            at += BLOCK
    return at


def first_kernel(*refs):
    query, refs = refs[0], refs[1:]
    others, piece, refs = refs[: POOL - 1], refs[POOL - 1], refs[POOL:]
    prepared, totals, peaks = refs[: POOL - 1], refs[POOL - 1 : 2 * POOL - 1], refs[2 * POOL - 1 : 3 * POOL - 1]
    keys, values = refs[3 * POOL - 1 :]
    key_count = load_pieces([piece], keys, values)
    for source, out in zip(others, prepared):
        prepare(source, out)
    for j, held in enumerate([query, *prepared]):
        for start in range(0, held.shape[0], ROW_TILE):
            rows = pl.ds(start, ROW_TILE)
            scores = scored(held[rows, :], keys[...])
            peak = spread(jnp.max(scores, axis=1, keepdims=True), ROW_TILE)
            weights = jnp.exp2(scores - wide(peak, key_count)).astype(bf16)
            totals[j][rows, :] = jnp.dot(weights, values[...], preferred_element_type=f32)
            peaks[j][rows, :] = peak


def first_fold(query, others, piece):
    rows, key_count = query.shape[0], piece.shape[0] * BLOCK
    shapes = (
        [jax.ShapeDtypeStruct((rows, 2 * HD), bf16)] * (POOL - 1)
        + [jax.ShapeDtypeStruct((rows, 2 * HD), f32)] * POOL
        + [jax.ShapeDtypeStruct((rows, HD), f32)] * POOL
    )
    outs = pl.pallas_call(
        first_kernel,
        out_shape=tuple(shapes),
        in_specs=[VMEM] * (POOL + 1),
        out_specs=(VMEM,) * len(shapes),
        scratch_shapes=[pltpu.VMEM((key_count, 2 * HD), bf16)] * 2,
        compiler_params=PARAMS,
        cost_estimate=cost(POOL * rows, key_count + 512),
    )(query, *others, piece)
    return [query, *outs[: POOL - 1]], list(outs[POOL - 1 : 2 * POOL - 1]), outs[2 * POOL - 1 :]


def add_tile(query, held, total, peak, keys, values, rows, start, length):
    span = pl.ds(start, length)
    weights = jnp.exp2(scored(query[rows, :], keys[span, :]) - wide(peak[rows, :], length))
    added = jnp.dot(weights.astype(bf16), values[span, :], preferred_element_type=f32)
    total[rows, :] = held[rows, :] + added


def fold_kernel(count, piece_count, looped, *refs):
    queries, peaks, refs = refs[:count], refs[count : 2 * count], refs[2 * count :]
    pieces, refs = refs[:piece_count], refs[piece_count:]
    totals, (keys, values) = refs[count : 2 * count], refs[2 * count :]
    key_count = load_pieces(pieces, keys, values)

    def add_all(held, key_start, length):
        for j in range(count):
            for start in range(0, queries[j].shape[0], ROW_TILE):
                rows = pl.ds(start, ROW_TILE)
                add_tile(queries[j], held[j], totals[j], peaks[j], keys, values, rows, key_start, length)

    def step(i, _):
        add_all(totals, pl.multiple_of(i * KEY_TILE, KEY_TILE), KEY_TILE)
        return 0

    if looped:
        for held, total in zip(refs[:count], totals):
            total[...] = held[...]
        lax.fori_loop(0, key_count // KEY_TILE, step, 0)
        rest = key_count % KEY_TILE
        if rest:
            add_all(totals, key_count - rest, rest)
    else:
        for key_start in range(0, key_count, KEY_TILE):
            length = min(KEY_TILE, key_count - key_start)
            add_all(totals if key_start else refs[:count], key_start, length)


def folded(queries, peaks, totals, pieces, looped=False):
    rows, count = queries[0].shape[0], len(queries)
    key_count = sum(p.shape[0] for p in pieces) * BLOCK
    at = 2 * count + len(pieces)
    return pl.pallas_call(
        lambda *refs: fold_kernel(count, len(pieces), looped, *refs),
        out_shape=(jax.ShapeDtypeStruct((rows, 2 * HD), f32),) * count,
        in_specs=[VMEM] * (at + count),
        out_specs=(VMEM,) * count,
        scratch_shapes=[pltpu.VMEM((key_count, 2 * HD), bf16)] * 2,
        input_output_aliases={at + j: j for j in range(count)},
        compiler_params=PARAMS,
        cost_estimate=cost(count * rows, key_count),
    )(*queries, *peaks, *pieces, *totals)


def refold(query, total, peak, blocks, every, semaphore):
    at = 0
    for piece in every:
        copy = pltpu.make_async_copy(piece, blocks.at[pl.ds(at, piece.shape[0])], semaphore)
        copy.start()
        copy.wait()
        at += piece.shape[0]
    total[...] = jnp.zeros_like(total)
    peak[...] = jnp.full(peak.shape, MASKED_SCORE, f32)
    ones = jnp.ones((BLOCK, HD), bf16)

    def step(i, _):
        b = i // (query.shape[0] // 64)
        rows = pl.ds(pl.multiple_of(i % (query.shape[0] // 64) * 64, 64), 64)
        key_rows = blocks[b, 0:BLOCK, :]
        scores = scored(query[rows, :], jnp.concatenate([key_rows, key_rows], axis=1))
        old = peak[rows, :]
        new = jnp.maximum(old, spread(jnp.max(scores, axis=1, keepdims=True), 64))
        weights = jnp.exp2(scores - new).astype(bf16)
        value_rows = jnp.concatenate([blocks[b, BLOCK : 2 * BLOCK, :], ones], axis=1)
        added = jnp.dot(weights, value_rows, preferred_element_type=f32)
        total[rows, :] = total[rows, :] * wide(jnp.exp2(old - new), 2 * HD) + added
        peak[rows, :] = new
        return 0

    lax.fori_loop(0, at * (query.shape[0] // 64), step, 0)


def last_kernel(piece_count, every_count, suffix_count, *refs):
    query, peak_in, total_in, refs = refs[0], refs[1], refs[2], refs[3:]
    suffix, refs = refs[:suffix_count], refs[suffix_count:]
    pieces, every, refs = refs[:piece_count], refs[piece_count:][:every_count], refs[piece_count + every_count :]
    out, total, peak, keys, values, blocks, semaphore = refs
    slots = out.shape[0]
    key_count = load_pieces(pieces, keys, values)
    peak[...] = peak_in[...]
    for key_start in range(0, key_count, KEY_TILE):
        for start in range(0, query.shape[0], ROW_TILE):
            length = min(KEY_TILE, key_count - key_start)
            held = total_in if key_start == 0 else total
            add_tile(query, held, total, peak_in, keys, values, pl.ds(start, ROW_TILE), key_start, length)

    @pl.when(jnp.logical_not(jnp.max(total[:, HD:]) < MASS_LIMIT))
    def _():
        refold(query, total, peak, blocks, every, semaphore)

    lane = lax.broadcasted_iota(jnp.int32, (slots, 128), 1)
    packed = jnp.zeros((slots, 128), f32)
    for h in range(H):
        rows = pl.ds(h * slots, slots)
        mass = total[rows, HD : 2 * HD]
        quotient = total[rows, 0:HD] / mass
        level = peak[rows, :] + jnp.log2(mass)
        if suffix:
            other, other_level = suffix[0][rows, :], suffix[1][rows, :]
            top = jnp.maximum(level, other_level)
            one, two = jnp.exp2(level - top), jnp.exp2(other_level - top)
            quotient = (one * quotient + two * other) / (one + two)
            level = top + jnp.log2(one + two)
        out[:, h * HD : (h + 1) * HD] = quotient.astype(bf16)
        one = level.astype(bf16).astype(f32)
        two = (level - one).astype(bf16).astype(f32)
        three = level - one - two
        term = jnp.where(lane % 16 == 0, one, jnp.where(lane % 16 == 1, two, three))
        packed = jnp.where((lane // 16 == h) & (lane % 16 < 3), term, packed)
    out[:, H * HD :] = packed.astype(bf16)


def last_fold(query, peak, total, pieces, every, suffix=()):
    rows = query.shape[0]
    slots = rows // H
    key_count = sum(p.shape[0] for p in pieces) * BLOCK
    block_count = sum(p.shape[0] for p in every)
    return pl.pallas_call(
        lambda *refs: last_kernel(len(pieces), len(every), len(suffix), *refs),
        out_shape=jax.ShapeDtypeStruct((slots, H * HD + 128), bf16),
        in_specs=[VMEM] * (3 + len(suffix) + len(pieces)) + [pl.BlockSpec(memory_space=pl.ANY)] * len(every),
        out_specs=VMEM,
        scratch_shapes=[
            pltpu.VMEM((rows, 2 * HD), f32),
            pltpu.VMEM((rows, HD), f32),
            pltpu.VMEM((key_count, 2 * HD), bf16),
            pltpu.VMEM((key_count, 2 * HD), bf16),
            pltpu.VMEM((block_count, 2 * BLOCK, HD), bf16),
            pltpu.SemaphoreType.DMA,
        ],
        compiler_params=PARAMS,
        cost_estimate=cost(rows, key_count),
    )(query, peak, total, *suffix, *pieces, *every)


def combine_kernel(*refs):
    parts, request, out = refs[:-2], *refs[-2:]
    slots = out.shape[0]
    own = request_column(request[...], slots)[0]
    live = jnp.broadcast_to(own < slots, (slots, HD))
    lane = lax.broadcasted_iota(jnp.int32, (128, H * HD), 0)
    column = lax.broadcasted_iota(jnp.int32, (128, H * HD), 1)
    gather = ((lane // 16 == column // HD) & (lane % 16 < 3)).astype(bf16)
    levels = [
        jnp.dot(part[:, H * HD :], gather, preferred_element_type=f32) for part in parts
    ]
    for h in range(H):
        columns = slice(h * HD, (h + 1) * HD)
        all_levels = [level[:, columns] for level in levels]
        all_quotients = [part[:, columns].astype(f32) for part in parts]
        top = all_levels[0]
        for level in all_levels[1:]:
            top = jnp.maximum(top, level)
        upper = lower = 0.0
        for level, quotient in zip(all_levels, all_quotients):
            weight = jnp.exp2(level - top)
            upper = upper + weight * quotient
            lower = lower + weight
        out[:, columns] = jnp.where(live, upper / lower, 0.0).astype(bf16)


def combined(parts, request_row):
    slots = parts[0].shape[0]
    return pl.pallas_call(
        combine_kernel,
        out_shape=jax.ShapeDtypeStruct((slots, H * HD), bf16),
        in_specs=[VMEM] * (len(parts) + 1),
        out_specs=VMEM,
        compiler_params=PARAMS,
    )(*parts, request_row)


def per_device(queries, suffix_keys, suffix_values, prefix_keys, prefix_values, slot_request):
    slots = queries.shape[0]
    request_row = slot_request.reshape(1, slots)
    own = jnp.concatenate([prefix_keys, prefix_values], axis=0)[None]

    far = [by_xor(own, dz=4), by_ring(own, dz=2), by_ring(own, dz=-2)]
    others = [
        by_xor(queries, dx=1, dz=1),
        by_xor(queries, dx=1),
        by_xor(queries, dz=1),
    ]
    first = jnp.concatenate([own, *far], axis=0)
    first, held_queries = lax.optimization_barrier((first, queries))
    query, *suffix = own_part(held_queries, suffix_keys, suffix_values, request_row)

    half_a, half_b = first[:2], first[2:]
    by_x = by_xor(first, dx=2)
    b_y = [by_ring(half_b, dy=1), by_ring(half_b, dy=-1), by_xor(half_b, dy=2)]
    by_x, *b_y = lax.optimization_barrier((by_x, *b_y))
    all_b_y = jnp.concatenate(b_y, axis=0)
    b_x = by_xor(all_b_y, dx=2)
    both_a = jnp.concatenate([half_a, by_x[:2]], axis=0)
    a_y = [by_ring(both_a, dy=1), by_ring(both_a, dy=-1), by_xor(both_a, dy=2)]
    pool, totals, peaks = first_fold(query, others, first)

    early = jnp.concatenate([first, by_x, all_b_y], axis=0)
    early, totals[0] = lax.optimization_barrier((early, totals[0]))
    early_c = by_xor(early, dc=1)
    totals = list(folded(pool, peaks, totals, [by_x, all_b_y], looped=True))
    totals = list(folded(pool, peaks, totals, [early_c], looped=True))
    *late, totals[0] = lax.optimization_barrier((*a_y, b_x, totals[0]))
    late_c = by_xor(jnp.concatenate(late, axis=0), dc=1)
    totals[1:] = folded(pool[1:], peaks[1:], totals[1:], late)

    every = [first, by_x, all_b_y, early_c, *late, late_c]
    parts = []
    for j in (1, 2, 3, 0):
        pieces = [late_c] if j else [*late, late_c]
        parts.append(last_fold(pool[j], peaks[j], totals[j], pieces, every, () if j else suffix))
    parts = [
        parts[3],
        by_xor(parts[0], dx=1, dz=1),
        by_xor(parts[1], dx=1),
        by_xor(parts[2], dz=1),
    ]
    return combined(parts, request_row)


def solution(mesh):
    placed = (
        P(AXES, None),
        P(AXES, None),
        P(AXES, None),
        P(AXES, None),
        P(AXES, None),
        P(AXES),
    )
    return jax.shard_map(
        per_device, mesh=mesh, in_specs=placed, out_specs=P(AXES, None), check_vma=False
    )
```
